512 devices in a mesh: region: 8 (over y, core), dom: 64 (over z, x).
Axes of the slice: x: 4, y: 4, z: 16, core: 2. Of those that a mesh axis runs over, the one named last changes fastest.
Arguments:
- flow_state: float32 [13312, 162], P(('region', 'dom')), may hold values from -6 to 6
- right_side: float32 [13312, 162], P(('region', 'dom')), may hold values from -6 to 6
- diag_block: bfloat16 [13312, 26244], P(('region', 'dom')), may hold values from -0.6 to 4.6
- face_scale: bfloat16 [13312, 4, 162], P(('region', 'dom')), may hold values from 0.25 to 2.5
- face_pattern: int32 [13312, 4], P(('region', 'dom')), may hold values from 0 to 5
- neighbour: int32 [13312, 4], P(('region', 'dom')), may hold values from -1 to 77, as said below
- templates: bfloat16 [54, 6, 162], replicated, may hold values from -0.875 to 0.875
- line_inverse: bfloat16 [32768, 26244], P(('region', 'dom')), may hold values from -0.25 to 1.25
- line_scale: bfloat16 [32768, 2, 162], P(('region', 'dom')), may hold values from 0.25 to 2.5
- line_pattern: int32 [32768, 2], P(('region', 'dom')), may hold values from 0 to 5
- elem_line: int32 [13312], P(('region', 'dom')), may hold values from 0 to 4095, as said below
Outputs:
- new_state: float32 [13312, 162], P(('region', 'dom'))
- residual: float32 [13312, 162], P(('region', 'dom'))
The draws below stay inside these ranges and needn't reach their ends.
Inputs may be any that keep to these rules, and one draw needn't show every extreme that they name: `elem_line`: value owner * 64 + line * 32 + position, owner in 0..63 within the element's region. Within a region every slot holds at most one element, and the filled positions of each line of 32 form a prefix of length 1 or more. The elements of one partition fill at most 1 slots of one line owner, reached in every draw; in every region some line owner has all 64 slots filled. -1 where a side has no neighbour; otherwise a row in three blocks of 26 elements: the partition of the same dom index in the previous region, the own partition, that of the next region. The neighbour meets the element with its opposite side.
All inputs are finite; a program needn't handle non-finite values.
Results may differ from the reference program's by a relative error of at most 0.0033.
Values may be sent and summed in bfloat16 or wider, within the bound.
A program may use at most 64 MiB of HBM per device.

```python
import math
import jax
import jax.numpy as jnp
from jax import lax

NV = 6
BLOCK = 162
TRACE = 54
NPAT = 6
LEN = 32
LPD = 2
ELEM_DEV = 26
SLOT_DEV = 64
GROUPS = 8
OWNERS = 64
ELEMS = 13312
SLOTS = 32768


def line_layout(key):
    owners = OWNERS
    keys = jax.random.split(key, 6)
    full_owner = jax.random.randint(keys[0], (), 0, owners)
    scores = jax.random.permutation(keys[1], owners)
    scores = scores.at[full_owner].set(owners)
    order_rank = jnp.argsort(jnp.argsort(scores, stable=True), stable=True).astype(jnp.int32)
    excess = SLOT_DEV - ELEM_DEV
    steady = excess // (owners - 1)
    leftover = excess % (owners - 1)
    baseline = ELEM_DEV - steady - (order_rank < leftover).astype(jnp.int32)
    margin = ELEM_DEV - steady - 3
    deltas = jax.random.randint(keys[2], (owners,), -margin, margin + 1)
    partner = jnp.bitwise_xor(order_rank, 1)
    paired = (partner <= owners - 2) & (order_rank <= owners - 2)
    signed = (1 - 2 * (order_rank % 2)) * deltas[order_rank // 2]
    loads = jnp.where(order_rank == owners - 1, SLOT_DEV, baseline + jnp.where(paired, signed, 0))
    lowest = jnp.maximum(1, loads - LEN)
    highest = jnp.minimum(LEN, loads - 1)
    first_len = lowest + jax.random.randint(keys[3], (owners,), 0, 1 << 20) % (highest - lowest + 1)
    lengths = jnp.stack([first_len, loads - first_len], axis=1)
    flat_len = lengths.reshape(-1)
    starts = (jnp.cumsum(flat_len) - flat_len).reshape(owners, 2)
    position = jnp.arange(LEN, dtype=jnp.int32)
    filled = position[None, None, :] < lengths[:, :, None]
    sequence = starts[:, :, None] + position[None, None, :]
    part_perm = jax.random.permutation(keys[4], owners).astype(jnp.int32)
    rotation = jax.random.randint(keys[5], (owners,), 0, ELEM_DEV)
    source = part_perm[sequence % owners]
    local_row = (sequence // owners + rotation[source]) % ELEM_DEV
    element = source * ELEM_DEV + local_row
    slot_id = jnp.arange(owners, dtype=jnp.int32)[:, None, None] * SLOT_DEV + jnp.arange(2, dtype=jnp.int32)[None, :, None] * LEN + position[None, None, :]
    target = jnp.where(filled, element, owners * ELEM_DEV).reshape(-1)
    return jnp.zeros((owners * ELEM_DEV,), jnp.int32).at[target].set(slot_id.reshape(-1).astype(jnp.int32), mode='drop')


def draw_elem_line(key, part):
    key = jax.random.fold_in(key, 11)
    region_ids = jnp.arange(GROUPS, dtype=jnp.int32)
    layouts = jax.vmap(lambda region: line_layout(jax.random.fold_in(key, region)))(region_ids)
    return layouts.reshape(-1).astype(jnp.int32)


def draw_neighbour(key, part):
    key = jax.random.fold_in(key, 5)
    keys = jax.random.split(key, 3)
    local_row = jnp.arange(ELEMS, dtype=jnp.int32) % ELEM_DEV
    selector = jax.random.randint(keys[0], (ELEMS, 4), 0, 10)
    picked = jax.random.randint(keys[1], (ELEMS, 4), 0, ELEM_DEV)
    others = (local_row[:, None] + 1 + jax.random.randint(keys[2], (ELEMS, 4), 0, ELEM_DEV - 1)) % ELEM_DEV
    inner = jnp.where(selector <= 4, 2 * ELEM_DEV + picked, ELEM_DEV + others)
    return jnp.where(selector == 0, -1, jnp.where(selector <= 2, picked, inner)).astype(jnp.int32)


def dominant_blocks(key, count, spread, low, high):
    key_off, key_diag = jax.random.split(key)
    scatter_part = spread * jax.random.truncated_normal(key_off, -4.0, 4.0, (count, BLOCK, BLOCK), jnp.float32)
    leading = jnp.exp(jax.random.uniform(key_diag, (count, BLOCK), jnp.float32, math.log(low), math.log(high)))
    identity = jnp.eye(BLOCK, dtype=jnp.float32)[None]
    return (scatter_part + leading[:, :, None] * identity).reshape(count, BLOCK * BLOCK)


def draw_diag_block(key, part):
    key = jax.random.fold_in(key, 7)
    return dominant_blocks(key, ELEMS, 0.6 / math.sqrt(BLOCK), 1.0, 4.0).astype(jnp.bfloat16)


def draw_line_inverse(key, part):
    key = jax.random.fold_in(key, 13)
    return dominant_blocks(key, SLOTS, 0.25 / math.sqrt(BLOCK), 0.5, 1.1).astype(jnp.bfloat16)


def with_ends(entries, key, least, largest):
    extent = entries.shape
    spot = [jax.random.randint(jax.random.fold_in(key, axis), (), 0, extent[axis]) for axis in range(len(extent))]
    entries = entries.at[tuple(spot)].set(least)
    longest = extent.index(max(extent))
    spot[longest] = (spot[longest] + 1) % extent[longest]
    return entries.at[tuple(spot)].set(largest)


def steps_of(stream_key, shape, pieces, smallest, top_value):
    gain, own = 1.0, jax.random.fold_in(stream_key, 6)
    for dim, parts in pieces:
        draws = jnp.exp(jax.random.uniform(jax.random.fold_in(own, dim), (parts,), jnp.float32, smallest / len(pieces), top_value / len(pieces)))
        gain = gain * jnp.repeat(draws, shape[dim] // parts).reshape([-1 if axis == dim else 1 for axis in range(len(shape))])
    return gain


def gaussian(stream_key, dims, scale, reach, pieces=(), kind=jnp.bfloat16):
    entries = scale * jax.random.normal(stream_key, dims, jnp.float32)
    if pieces:
        entries = entries * steps_of(stream_key, dims, pieces, -0.22, 0.18)
    return jnp.clip(entries, -reach, reach).astype(kind)


def setup_inputs(seed: int = 0) -> dict:
    splits = jax.random.split(jax.random.key(seed), 12)
    flow_state = gaussian(splits[0], (ELEMS, BLOCK), 1.0, 6.0, ((0, 512),), jnp.float32)
    right_side = gaussian(splits[1], (ELEMS, BLOCK), 1.0, 6.0, ((0, 512),), jnp.float32)
    diag_block = draw_diag_block(jax.random.fold_in(splits[11], 71), 0)
    face_scale = jnp.clip(jnp.exp(math.log(2.5) - 2.3025851 * jax.random.uniform(splits[3], (ELEMS, 4, BLOCK), jnp.float32) ** steps_of(splits[3], (ELEMS, 4, BLOCK), ((0, 512),), -0.2, 0.2)), 0.25, 2.5).astype(jnp.bfloat16)
    face_pattern = with_ends(jax.random.randint(splits[4], (ELEMS, 4), 0, NPAT), jax.random.fold_in(splits[4], 1), 0, NPAT - 1).astype(jnp.int32)
    neighbour = draw_neighbour(jax.random.fold_in(splits[11], 71), 0)
    templates = gaussian(splits[6], (TRACE, NPAT, BLOCK), TRACE ** -0.5, 0.875)
    line_inverse = draw_line_inverse(jax.random.fold_in(splits[11], 71), 0)
    line_scale = jnp.clip(jnp.exp(math.log(2.5) - 2.3025851 * jax.random.uniform(splits[8], (SLOTS, 2, BLOCK), jnp.float32) ** steps_of(splits[8], (SLOTS, 2, BLOCK), ((0, 512),), -0.2, 0.2)), 0.25, 2.5).astype(jnp.bfloat16)
    line_pattern = with_ends(jax.random.randint(splits[9], (SLOTS, 2), 0, NPAT), jax.random.fold_in(splits[9], 1), 0, NPAT - 1).astype(jnp.int32)
    elem_line = draw_elem_line(jax.random.fold_in(splits[11], 71), 0)
    return {"flow_state": flow_state, "right_side": right_side, "diag_block": diag_block, "face_scale": face_scale, "face_pattern": face_pattern, "neighbour": neighbour, "templates": templates, "line_inverse": line_inverse, "line_scale": line_scale, "line_pattern": line_pattern, "elem_line": elem_line}


HIGHEST = lax.Precision.HIGHEST
OPPOSITE = (1, 0, 3, 2)


def face_trace(values, face_id):
    nodal = values.reshape(values.shape[:-1] + (NV, 3, 3, 3))
    if face_id == 0:
        picked = nodal[..., 0, :, :]
    elif face_id == 1:
        picked = nodal[..., 2, :, :]
    elif face_id == 2:
        picked = nodal[..., :, 0, :]
    elif face_id == 3:
        picked = nodal[..., :, 2, :]
    elif face_id == 4:
        picked = nodal[..., 0]
    else:
        picked = nodal[..., 2]
    return picked.reshape(values.shape[:-1] + (NV * 9,))


def apply_patterns(traces, patterns, templates):
    all_terms = jnp.einsum('na,apb->npb', traces.astype(jnp.float32), templates.astype(jnp.float32), precision=HIGHEST)
    select = (patterns[:, None] == jnp.arange(NPAT, dtype=jnp.int32)[None, :]).astype(jnp.float32)
    return jnp.sum(select[:, :, None] * all_terms, axis=1)


def reference(flow_state, right_side, diag_block, face_scale, face_pattern, neighbour, templates, line_inverse, line_scale, line_pattern, elem_line):
    devices = GROUPS * OWNERS
    rounded = lax.optimization_barrier(flow_state.astype(jnp.bfloat16))
    row_ids = jnp.arange(ELEMS, dtype=jnp.int32)
    group_of = row_ids // (OWNERS * ELEM_DEV)
    part_of = (row_ids // ELEM_DEV) % OWNERS
    target_group = group_of[:, None] + neighbour // ELEM_DEV - 1
    present = (neighbour >= 0) & (target_group >= 0) & (target_group < GROUPS)
    source = (target_group * OWNERS + part_of[:, None]) * ELEM_DEV + neighbour % ELEM_DEV
    fetched = rounded[jnp.clip(source, 0, ELEMS - 1)]
    far_traces = jnp.stack([face_trace(fetched[:, face_index], OPPOSITE[face_index]) for face_index in range(4)], axis=1)

    def element_terms(inputs):
        block, states, traces, gates, patterns, scales, given = inputs
        own_term = jnp.einsum('ebc,ec->eb', block.astype(jnp.float32), states.astype(jnp.float32), precision=HIGHEST)
        coupled = apply_patterns(traces.reshape(-1, TRACE), patterns.reshape(-1), templates).reshape(ELEM_DEV, 4, BLOCK)
        coupled = coupled * scales.astype(jnp.float32) * gates[:, :, None]
        return given - own_term - jnp.sum(coupled, axis=1)

    partial_value = lax.map(element_terms, (
        diag_block.reshape(devices, ELEM_DEV, BLOCK, BLOCK),
        rounded.reshape(devices, ELEM_DEV, BLOCK),
        far_traces.reshape(devices, ELEM_DEV, 4, TRACE),
        present.astype(jnp.float32).reshape(devices, ELEM_DEV, 4),
        face_pattern.reshape(devices, ELEM_DEV, 4),
        face_scale.reshape(devices, ELEM_DEV, 4, BLOCK),
        right_side.reshape(devices, ELEM_DEV, BLOCK))).reshape(ELEMS, BLOCK)

    global_slot = group_of * (OWNERS * SLOT_DEV) + elem_line
    slot_elem = jnp.full((SLOTS,), -1, jnp.int32).at[global_slot].set(row_ids)
    filled = slot_elem >= 0
    chosen_rows = jnp.clip(slot_elem, 0, ELEMS - 1)
    line_states = jnp.where(filled[:, None], rounded[chosen_rows], jnp.zeros((), jnp.bfloat16))
    line_partial = jnp.where(filled[:, None], partial_value[chosen_rows], jnp.zeros((), jnp.float32))
    line_count = SLOTS // LEN
    filled_lines = filled.reshape(line_count, LEN)
    position = jnp.arange(LEN, dtype=jnp.int32)
    lower_on = (filled_lines & (position[None, :] > 0)).astype(jnp.float32).reshape(-1)
    upper_on = jnp.concatenate([filled_lines[:, 1:], jnp.zeros((line_count, 1), bool)], axis=1).astype(jnp.float32).reshape(-1)
    top_traces = face_trace(line_states, 5).reshape(line_count, LEN, TRACE)
    bottom_traces = face_trace(line_states, 4).reshape(line_count, LEN, TRACE)
    prev_tops = jnp.concatenate([jnp.zeros_like(top_traces[:, :1]), top_traces[:, :-1]], axis=1).reshape(SLOTS, TRACE)
    next_bottoms = jnp.concatenate([bottom_traces[:, 1:], jnp.zeros_like(bottom_traces[:, :1])], axis=1).reshape(SLOTS, TRACE)
    scales = line_scale.astype(jnp.float32)
    lower_term = apply_patterns(prev_tops, line_pattern[:, 0], templates) * scales[:, 0] * lower_on[:, None]
    upper_term = apply_patterns(next_bottoms, line_pattern[:, 1], templates) * scales[:, 1] * upper_on[:, None]
    line_rhs = line_partial - lower_term - upper_term

    def solve_lines(inputs):
        inverse, given, lower_scale, upper_scale, lower_kind, upper_kind = inputs
        inverse_lines = inverse.reshape(LPD, LEN, BLOCK, BLOCK)
        given = given.reshape(LPD, LEN, BLOCK)
        lower_scale = lower_scale.reshape(LPD, LEN, BLOCK)
        upper_scale = upper_scale.reshape(LPD, LEN, BLOCK)
        lower_kind = lower_kind.reshape(LPD, LEN)
        upper_kind = upper_kind.reshape(LPD, LEN)

        def forward(prev_top, place):
            blocks = lax.dynamic_index_in_dim(inverse_lines, place, 1, keepdims=False).astype(jnp.float32)
            coupling = lax.dynamic_index_in_dim(lower_scale, place, 1, keepdims=False) * apply_patterns(prev_top, lax.dynamic_index_in_dim(lower_kind, place, 1, keepdims=False), templates)
            forced = lax.dynamic_index_in_dim(given, place, 1, keepdims=False) - coupling
            solved = jnp.einsum('lbc,lc->lb', blocks, forced, precision=HIGHEST)
            return face_trace(solved, 5), solved

        _, sweep_out = lax.scan(forward, jnp.zeros((LPD, TRACE), jnp.float32), position)
        interim = jnp.swapaxes(sweep_out, 0, 1)

        def backward(next_bottom, place):
            blocks = lax.dynamic_index_in_dim(inverse_lines, place, 1, keepdims=False).astype(jnp.float32)
            coupling = lax.dynamic_index_in_dim(upper_scale, place, 1, keepdims=False) * apply_patterns(next_bottom, lax.dynamic_index_in_dim(upper_kind, place, 1, keepdims=False), templates)
            corrected = lax.dynamic_index_in_dim(interim, place, 1, keepdims=False) - jnp.einsum('lbc,lc->lb', blocks, coupling, precision=HIGHEST)
            return face_trace(corrected, 4), corrected

        _, back_out = lax.scan(backward, jnp.zeros((LPD, TRACE), jnp.float32), position, reverse=True)
        return jnp.swapaxes(back_out, 0, 1).reshape(SLOT_DEV, BLOCK)

    corrections = lax.map(solve_lines, (
        line_inverse.reshape(devices, SLOT_DEV, BLOCK, BLOCK),
        line_rhs.reshape(devices, SLOT_DEV, BLOCK),
        (scales[:, 0] * lower_on[:, None]).reshape(devices, SLOT_DEV, BLOCK),
        (scales[:, 1] * upper_on[:, None]).reshape(devices, SLOT_DEV, BLOCK),
        line_pattern[:, 0].reshape(devices, SLOT_DEV),
        line_pattern[:, 1].reshape(devices, SLOT_DEV))).reshape(SLOTS, BLOCK)
    return flow_state + corrections[global_slot], line_rhs[global_slot]
```

```python
import functools

import jax
import jax.numpy as jnp
import numpy as np
from jax import lax
from jax.experimental import pallas as pl
from jax.experimental.pallas import tpu as pltpu
from jax.sharding import PartitionSpec as P

MESH = pl.DeviceIdType.MESH
F32, BF16 = jnp.float32, jnp.bfloat16
HIGHEST = lax.Precision.HIGHEST
OPPOSITE = (1, 0, 3, 2)

NV = 6
NPAT = 6
LEN = 32
BLOCK = 162
TRACE = 54
ELEM = 26
SLOTS = 64
EROWS = 32
WIDE = 256
TSTEP = 64
TALL = NPAT * TSTEP
MROWS = 56
MSG = 384


def trace_rows(face_id):
    rows = np.arange(BLOCK).reshape(NV, 3, 3, 3)
    a, b, c = (slice(None),) * 3
    if face_id < 2:
        a = 2 * face_id
    elif face_id < 4:
        b = 2 * (face_id - 2)
    else:
        c = 2 * (face_id - 4)
    return rows[:, a, b, c].reshape(-1)


def trace_picks():
    picks = np.zeros((4, WIDE, TALL), np.float32)
    for side in range(4):
        rows = trace_rows(OPPOSITE[side])
        for pattern in range(NPAT):
            picks[side, rows, pattern * TSTEP + np.arange(TRACE)] = 1.0
    return picks


def line_picks():
    picks = np.zeros((WIDE, 128), np.float32)
    picks[trace_rows(5), np.arange(TRACE)] = 1.0
    picks[trace_rows(4), TSTEP + np.arange(TRACE)] = 1.0
    return picks


def dot(a, b, **kw):
    return jnp.dot(a, b, preferred_element_type=F32, **kw)


def lanes(rows, width):
    return lax.broadcasted_iota(jnp.int32, (rows, width), 1)


def halves(x):
    high = x.astype(BF16)
    return high, (x - high.astype(F32)).astype(BF16)


def block_row(ref, rows, start, stop):
    base = pl.multiple_of((start // 128) * 128, 128)
    shift = lax.rem(128 - (start - base), 128)
    tiles = [ref[0:rows, pl.ds(pl.multiple_of(base + 128 * t, 128), 128)].astype(F32) for t in range(3)]
    moved = [pltpu.roll(tile, shift, 1) for tile in tiles]
    keep = lanes(rows, 128) < 128 - (start - base)
    return jnp.concatenate([jnp.where(keep, moved[0], moved[1]), jnp.where(keep, moved[1], moved[2])], axis=1)


def lane_sums(product):
    return jnp.sum(product[:, 0:128] + product[:, 128:256], axis=1, keepdims=True)


def masked_terms(x, patterns, gate, table):
    spread = jnp.concatenate([x, x, x], axis=1)
    rows = x.shape[0]
    spread = jnp.where((lanes(rows, TALL) // TSTEP).astype(F32) == patterns, spread * gate, 0.0)
    return spread


def kernel(
    groups,
    owners,
    fs_ref,
    rs_ref,
    diag_hbm,
    fsc_ref,
    fp_ref,
    nb_ref,
    tmpl_ref,
    linv_hbm,
    lsc_ref,
    lp_ref,
    el_ref,
    picks_ref,
    lpick_ref,
    ns_out,
    res_out,
    diag,
    linv,
    ints,
    xs,
    st,
    tf,
    tp,
    slab,
    mm,
    nn,
    kk,
    own,
    gg,
    hh,
    ff,
    bb,
    cc,
    rhs_s,
    send,
    recv,
    back,
    ret,
    dsem,
    ssem,
    rsem,
):
    reg = lax.axis_index("region")
    me = lax.axis_index("dom")

    bar = pltpu.get_barrier_semaphore()
    below, above = lax.rem(reg + groups - 1, groups), lax.rem(reg + 1, groups)

    def greet(i, carry):
        pl.semaphore_signal(bar, inc=1, device_id=(reg, lax.rem(me + i, owners)), device_id_type=MESH)
        return carry

    pl.semaphore_signal(bar, inc=1, device_id=(below, me), device_id_type=MESH)
    pl.semaphore_signal(bar, inc=1, device_id=(above, me), device_id_type=MESH)
    lax.fori_loop(1, owners, greet, 0)
    get_diag = pltpu.make_async_copy(diag_hbm, diag, dsem.at[0])
    get_linv = pltpu.make_async_copy(linv_hbm, linv, dsem.at[1])
    get_diag.start()
    get_linv.start()

    ints[...] = jnp.full((16, 128), -1.0, F32)
    ints[0:4, 0:ELEM] = nb_ref[...].astype(F32)
    ints[4:8, 0:ELEM] = fp_ref[...].astype(F32)
    ints[8:9, 0:ELEM] = el_ref[...].astype(F32)
    ints[9:11, 0:SLOTS] = lp_ref[...].astype(F32)
    columns = jnp.transpose(ints[...])

    xs[...] = jnp.zeros((EROWS, WIDE), F32)
    xs[0:ELEM, 0:BLOCK] = fs_ref[...]
    rounded = xs[...].astype(BF16)
    st[1] = rounded
    wide_state = rounded.astype(F32)

    tf[...] = jnp.zeros((TALL, WIDE), F32)
    for pattern in range(NPAT):
        tf[pattern * TSTEP : pattern * TSTEP + TRACE, 0:BLOCK] = tmpl_ref[pattern].astype(F32)
    tp[...] = tf[...].astype(BF16)

    get_diag.wait()
    own[...] = jnp.zeros((EROWS, WIDE), F32)
    elem_lane = lanes(ELEM, WIDE)

    def own_rows(b, carry):
        value = lane_sums(block_row(diag, ELEM, b * BLOCK, None) * wide_state[0:ELEM])
        own[0:ELEM] = jnp.where(elem_lane == b, value, own[0:ELEM])
        return carry

    lax.fori_loop(0, BLOCK - 1, own_rows, 0)
    tail = diag[:, (BLOCK - 1) * BLOCK - 98 : BLOCK * BLOCK].astype(F32)
    xs[0:ELEM, 0:BLOCK] = tail[:, 98 : 98 + BLOCK]
    value = lane_sums(xs[...] * wide_state)
    own[...] = jnp.where(lanes(EROWS, WIDE) == BLOCK - 1, value, own[...])

    pl.semaphore_wait(bar, owners + 1)
    up = pltpu.make_async_remote_copy(
        src_ref=st.at[1], dst_ref=st.at[0], send_sem=ssem.at[0], recv_sem=rsem.at[0], device_id=(above, me), device_id_type=MESH
    )
    down = pltpu.make_async_remote_copy(
        src_ref=st.at[1], dst_ref=st.at[2], send_sem=ssem.at[1], recv_sem=rsem.at[1], device_id=(below, me), device_id_type=MESH
    )
    up.start()
    down.start()
    up.wait()
    down.wait()

    stacked = jnp.concatenate([st[0], st[1], st[2]], axis=0)
    row_lane = lanes(EROWS, 3 * EROWS).astype(F32)
    has_below = jnp.where(reg > 0, 1.0, 0.0)
    has_above = jnp.where(reg < groups - 1, 1.0, 0.0)
    pieces = []
    for side in range(4):
        near = columns[0:EROWS, side : side + 1]
        part = jnp.where(near >= ELEM, 1.0, 0.0) + jnp.where(near >= 2 * ELEM, 1.0, 0.0)
        place = near + (EROWS - ELEM) * part
        present = jnp.where(part == 0.0, has_below, jnp.where(part == 2.0, has_above, 1.0))
        pick = jnp.where(row_lane == place, present, 0.0).astype(BF16)
        fetched = dot(pick, stacked).astype(BF16)
        spread = dot(fetched, picks_ref[side])
        pattern = columns[0:EROWS, 4 + side : 5 + side]
        pieces.append(jnp.where((lanes(EROWS, TALL) // TSTEP).astype(F32) == pattern, spread, 0.0).astype(BF16))
    terms = dot(jnp.concatenate(pieces, axis=0), tp[...])
    total = own[...]
    for side in range(4):
        total = total + terms[side * EROWS : (side + 1) * EROWS] * fsc_ref[side]
    xs[...] = jnp.zeros((EROWS, WIDE), F32)
    xs[0:ELEM, 0:BLOCK] = rs_ref[...]
    partial = xs[...] - total

    slot = columns[0:EROWS, 8:9]
    owner = jnp.floor(slot * (1.0 / SLOTS))
    local_slot = slot - owner * SLOTS
    traces = dot(rounded, lpick_ref[...])
    traces = jnp.where(lanes(EROWS, 128) == 127, local_slot + 1.0, traces)
    owner_row = jnp.floor(ints[8:9, 0:EROWS] * (1.0 / SLOTS))
    pick_owner = jnp.where(lax.broadcasted_iota(jnp.int32, (owners, EROWS), 0).astype(F32) == owner_row, 1.0, 0.0)
    payload = jnp.concatenate([traces, partial], axis=1)
    send[:, 0, :] = dot(pick_owner, payload, precision=HIGHEST)

    def exchange(source, target, index):
        def one(i, carry):
            other = lax.rem(me + i, owners)
            pltpu.make_async_remote_copy(
                src_ref=source.at[other],
                dst_ref=target.at[me],
                send_sem=ssem.at[index],
                recv_sem=rsem.at[index],
                device_id=(reg, other),
                device_id_type=MESH,
            ).start()
            return carry

        lax.fori_loop(1, owners, one, 0)
        target[pl.ds(me, 1)] = source[pl.ds(me, 1)]

    def finish(source, target, index):
        whole = pltpu.make_async_remote_copy(
            src_ref=source.at[pl.ds(0, owners - 1)],
            dst_ref=target.at[pl.ds(0, owners - 1)],
            send_sem=ssem.at[index],
            recv_sem=rsem.at[index],
            device_id=(reg, lax.rem(me + 1, owners)),
            device_id_type=MESH,
        )
        whole.wait_send()
        whole.wait_recv()

    exchange(send, recv, 2)

    get_linv.wait()

    def rows_of(b, carry):
        slab[b] = block_row(linv, SLOTS, b * BLOCK, None)
        return carry

    lax.fori_loop(0, BLOCK - 1, rows_of, 0)
    tail = linv[:, (BLOCK - 1) * BLOCK - 98 : BLOCK * BLOCK].astype(F32)
    slab[BLOCK - 1] = jnp.zeros((SLOTS, WIDE), F32)
    slab[BLOCK - 1, :, 0:BLOCK] = tail[:, 98 : 98 + BLOCK]

    kinds = [columns[0:SLOTS, 9 + i : 10 + i] for i in range(2)]
    chosen = [jnp.where((lanes(SLOTS, TALL) // TSTEP).astype(F32) == kind, 1.0, 0.0) for kind in kinds]
    low_half = lanes(SLOTS, 128) < TSTEP

    def small_rows(m, carry):
        first, last = slab[3 * m], slab[3 * m + 2]
        scaled = [last * lsc_ref[0], first * lsc_ref[0], first * lsc_ref[1]]
        parts = [halves(x) for x in scaled]
        stack = jnp.concatenate([p[0] for p in parts] + [p[1] for p in parts], axis=0)
        product = lax.dot_general(stack, tp[...], (((1,), (1,)), ((), ())), preferred_element_type=F32)
        product = product[0 : 3 * SLOTS] + product[3 * SLOTS :]
        for i, (target, kind) in enumerate(((mm, 0), (kk, 0), (nn, 1))):
            x = product[i * SLOTS : (i + 1) * SLOTS] * chosen[kind]
            x = x[:, 0:128] + x[:, 128:256] + x[:, 256:384]
            x = jnp.where(low_half, x + pltpu.roll(x, TSTEP, 1), 0.0)
            if target is kk:
                kk[m] = x
            else:
                target[pl.ds(m, SLOTS, stride=MROWS), :] = x
        return carry

    lax.fori_loop(0, TRACE, small_rows, 0)
    for m in range(TRACE, MROWS):
        mm[pl.ds(m, SLOTS, stride=MROWS), :] = jnp.zeros((SLOTS, 128), F32)
        nn[pl.ds(m, SLOTS, stride=MROWS), :] = jnp.zeros((SLOTS, 128), F32)

    finish(send, recv, 2)
    got = recv[:, 0, :]
    slot_column = got[:, 127:128] - 1.0
    to_slot = jnp.where(lanes(owners, SLOTS).astype(F32) == slot_column, 1.0, 0.0)
    from_source = jnp.transpose(to_slot)
    gathered = dot(from_source, got, precision=HIGHEST)
    filled = jnp.sum(from_source, axis=1, keepdims=True)
    place = lax.rem(lax.broadcasted_iota(jnp.int32, (SLOTS, 1), 0), LEN)
    lower = jnp.where(place > 0, filled, 0.0)
    upper = jnp.where(place < LEN - 1, pltpu.roll(jnp.broadcast_to(filled, (SLOTS, 128)), SLOTS - 1, 0)[:, 0:1], 0.0)

    def coupled(traces_before, traces_after):
        spreads = []
        for x, kind, gate in ((traces_before, 0, lower), (traces_after, 1, upper)):
            x = jnp.where(low_half & (gate > 0.5), x, 0.0)
            x = x + pltpu.roll(x, TSTEP, 1)
            spreads.append(jnp.concatenate([x, x, x], axis=1) * chosen[kind])
        x = jnp.concatenate(spreads, axis=0)
        high, low = halves(x)
        terms = dot(jnp.concatenate([high, low], axis=0), tp[...])
        terms = terms[0 : 2 * SLOTS] + terms[2 * SLOTS :]
        return terms[0:SLOTS] * lsc_ref[0] + terms[SLOTS:] * lsc_ref[1]

    line_traces = gathered[:, 0:128]
    tops = pltpu.roll(line_traces, 1, 0)
    bottoms = pltpu.roll(pltpu.roll(line_traces, TSTEP, 1), SLOTS - 1, 0)
    rhs = gathered[:, 128:384] - coupled(tops, bottoms)
    rhs_s[...] = rhs

    slot_lane = lanes(SLOTS, 128)
    gg[...] = jnp.zeros((SLOTS, 128), F32)
    hh[...] = jnp.zeros((SLOTS, 128), F32)

    def ends(m, carry):
        given = rhs_s[...]
        gg[...] = jnp.where(slot_lane == m, lane_sums(slab[3 * m + 2] * given), gg[...])
        hh[...] = jnp.where(slot_lane == m, lane_sums(slab[3 * m] * given), hh[...])
        return carry

    lax.fori_loop(0, TRACE, ends, 0)

    eye = jnp.where(lanes(MROWS, 128) == lax.broadcasted_iota(jnp.int32, (MROWS, 128), 0), 1.0, 0.0)

    def sweep(matrices, given, out, reverse):
        def step(i, carry):
            position = LEN - 1 - i if reverse else i
            after = []
            for line in range(2):
                j = line * LEN + position
                matrix = matrices[pl.ds(pl.multiple_of(j * MROWS, 8), MROWS), :]
                column = jnp.sum(matrix * carry[line], axis=1, keepdims=True)
                row = given[pl.ds(j, 1), :] - jnp.sum(eye * column, axis=0, keepdims=True)
                out[pl.ds(j, 1), :] = row
                after.append(row)
            return tuple(after)

        zero = jnp.zeros((1, 128), F32)
        lax.fori_loop(0, LEN, step, (zero, zero))

    sweep(mm, gg, ff, False)
    before = jnp.where(lower > 0.5, pltpu.roll(ff[...], 1, 0), 0.0)
    ff[...] = before

    def reduce_first(m, carry):
        hh[...] = jnp.where(slot_lane == m, hh[...] - jnp.sum(kk[m] * ff[...], axis=1, keepdims=True), hh[...])
        return carry

    lax.fori_loop(0, TRACE, reduce_first, 0)
    hh[...] = jnp.where(filled > 0.5, hh[...], 0.0)
    sweep(nn, hh, bb, True)
    after = jnp.where(upper > 0.5, pltpu.roll(bb[...], SLOTS - 1, 0), 0.0)
    cc[...] = rhs_s[...] - coupled(before, after)

    send_lane = lanes(SLOTS, WIDE)
    ret[...] = jnp.zeros((SLOTS, WIDE), F32)

    def solve(b, carry):
        ret[...] = jnp.where(send_lane == b, lane_sums(slab[b] * cc[...]), ret[...])
        return carry

    lax.fori_loop(0, BLOCK, solve, 0)
    both = jnp.concatenate([ret[...], rhs_s[...]], axis=1)
    answer = dot(to_slot, both, precision=HIGHEST)
    send[:, 0, :] = jnp.concatenate([answer[:, 0:128], answer[:, 256:384], jnp.where(slot_lane < TSTEP, answer[:, 128:256], pltpu.roll(answer[:, 384:512], TSTEP, 1))], axis=1)
    exchange(send, back, 3)
    finish(send, back, 3)
    answer = dot(jnp.transpose(pick_owner), back[:, 0, :], precision=HIGHEST)
    third = answer[:, 256:384]
    fixed = jnp.concatenate([answer[:, 0:128], third], axis=1)
    kept = jnp.concatenate([answer[:, 128:256], pltpu.roll(third, TSTEP, 1)], axis=1)
    ns_out[...] = fs_ref[...] + fixed[0:ELEM, 0:BLOCK]
    res_out[...] = kept[0:ELEM, 0:BLOCK]


def local(groups, owners, flow_state, right_side, diag_block, face_scale, face_pattern, neighbour, templates, line_inverse, line_scale, line_pattern, elem_line):
    face_scales = jnp.pad(jnp.transpose(face_scale, (1, 0, 2)).astype(F32), ((0, 0), (0, EROWS - ELEM), (0, WIDE - BLOCK)))
    line_scales = jnp.pad(jnp.transpose(line_scale, (1, 0, 2)).astype(F32), ((0, 0), (0, 0), (0, WIDE - BLOCK)))
    operands = (
        flow_state,
        right_side,
        diag_block,
        face_scales,
        face_pattern.T,
        neighbour.T,
        jnp.transpose(templates, (1, 0, 2)),
        line_inverse,
        line_scales,
        line_pattern.T,
        elem_line[None, :],
        jnp.asarray(trace_picks(), BF16),
        jnp.asarray(line_picks(), BF16),
    )
    vmem = pl.BlockSpec(memory_space=pltpu.VMEM)
    anywhere = pl.BlockSpec(memory_space=pl.ANY)
    message = pltpu.VMEM((owners, 1, MSG), F32)
    return pl.pallas_call(
        functools.partial(kernel, groups, owners),
        out_shape=(jax.ShapeDtypeStruct((ELEM, BLOCK), F32), jax.ShapeDtypeStruct((ELEM, BLOCK), F32)),
        in_specs=[vmem, vmem, anywhere, vmem, vmem, vmem, vmem, anywhere, vmem, vmem, vmem, vmem, vmem],
        out_specs=(vmem, vmem),
        scratch_shapes=[
            pltpu.VMEM((ELEM, BLOCK * BLOCK), BF16),
            pltpu.VMEM((SLOTS, BLOCK * BLOCK), BF16),
            pltpu.VMEM((16, 128), F32),
            pltpu.VMEM((EROWS, WIDE), F32),
            pltpu.VMEM((3, EROWS, WIDE), BF16),
            pltpu.VMEM((TALL, WIDE), F32),
            pltpu.VMEM((TALL, WIDE), BF16),
            pltpu.VMEM((BLOCK, SLOTS, WIDE), F32),
            pltpu.VMEM((SLOTS * MROWS, 128), F32),
            pltpu.VMEM((SLOTS * MROWS, 128), F32),
            pltpu.VMEM((TRACE, SLOTS, 128), F32),
            pltpu.VMEM((EROWS, WIDE), F32),
            pltpu.VMEM((SLOTS, 128), F32),
            pltpu.VMEM((SLOTS, 128), F32),
            pltpu.VMEM((SLOTS, 128), F32),
            pltpu.VMEM((SLOTS, 128), F32),
            pltpu.VMEM((SLOTS, WIDE), F32),
            pltpu.VMEM((SLOTS, WIDE), F32),
            message,
            message,
            message,
            pltpu.VMEM((SLOTS, WIDE), F32),
            pltpu.SemaphoreType.DMA((2,)),
            pltpu.SemaphoreType.DMA((4,)),
            pltpu.SemaphoreType.DMA((4,)),
        ],
        compiler_params=pltpu.CompilerParams(collective_id=0, has_side_effects=True, vmem_limit_bytes=56 * 1024 * 1024),
    )(*operands)


def solution(mesh):
    both = ("region", "dom")
    return jax.shard_map(
        functools.partial(local, mesh.shape["region"], mesh.shape["dom"]),
        mesh=mesh,
        in_specs=(
            P(both, None),
            P(both, None),
            P(both, None),
            P(both, None, None),
            P(both, None),
            P(both, None),
            P(),
            P(both, None),
            P(both, None, None),
            P(both, None),
            P(both),
        ),
        out_specs=(P(both, None), P(both, None)),
        check_vma=False,
    )
```

```python
import functools

import jax
import jax.numpy as jnp
import numpy as np
from jax import lax
from jax.experimental import pallas as pl
from jax.experimental.pallas import tpu as pltpu
from jax.sharding import PartitionSpec as P

MESH = pl.DeviceIdType.MESH
F32, BF16 = jnp.float32, jnp.bfloat16
HIGHEST = lax.Precision.HIGHEST
OPPOSITE = (1, 0, 3, 2)

NV = 6
NPAT = 6
LEN = 32
BLOCK = 162
TRACE = 54
ELEM = 26
SLOTS = 64
EROWS = 32
WIDE = 256
TSTEP = 64
TALL = NPAT * TSTEP
MROWS = 56
MSG = 384


def trace_column(face_id, width):
    k = lax.rem(lanes(1, width), TSTEP).astype(F32)
    variable, rest = jnp.floor((k + 0.5) * (1.0 / 9.0)), 0.0
    line = jnp.floor((k + 0.5) * (1.0 / 3.0))
    if face_id < 2:
        rest = k + 18.0 * variable + 18.0 * face_id
    elif face_id < 4:
        rest = k + 6.0 * line + 6.0 * (face_id - 2)
    else:
        rest = 3.0 * k + 2.0 * (face_id - 4)
    return jnp.where(k < TRACE, rest, -1.0)


def picks_of(column):
    rows = lax.broadcasted_iota(jnp.int32, (WIDE, column.shape[1]), 0).astype(F32)
    return jnp.where(rows == column, 1.0, 0.0).astype(BF16)


def dot(a, b, **kw):
    return jnp.dot(a, b, preferred_element_type=F32, **kw)


def lanes(rows, width):
    return lax.broadcasted_iota(jnp.int32, (rows, width), 1)


def halves(x):
    high = x.astype(BF16)
    return high, (x - high.astype(F32)).astype(BF16)


def block_row(ref, rows, start):
    base = pl.multiple_of((start // 128) * 128, 128)
    shift = lax.rem(128 - (start - base), 128)
    tiles = [ref[0:rows, pl.ds(pl.multiple_of(base + 128 * t, 128), 128)].astype(F32) for t in range(3)]
    moved = [pltpu.roll(tile, shift, 1) for tile in tiles]
    keep = lanes(rows, 128) < 128 - (start - base)
    return jnp.concatenate([jnp.where(keep, moved[0], moved[1]), jnp.where(keep, moved[1], moved[2])], axis=1)


def lane_sums(product):
    return jnp.sum(product[:, 0:128] + product[:, 128:256], axis=1, keepdims=True)


def masked_terms(x, patterns, gate, table):
    spread = jnp.concatenate([x, x, x], axis=1)
    rows = x.shape[0]
    spread = jnp.where((lanes(rows, TALL) // TSTEP).astype(F32) == patterns, spread * gate, 0.0)
    return spread


def kernel(
    groups,
    owners,
    fs_hbm,
    rs_hbm,
    diag_hbm,
    fsc_hbm,
    fp_hbm,
    nb_hbm,
    tmpl_hbm,
    linv_hbm,
    lsc_hbm,
    lp_hbm,
    el_hbm,
    ns_out,
    res_out,
    fs_ref,
    rs_ref,
    fsc_ref,
    fp_ref,
    nb_ref,
    tmpl_ref,
    lsc_ref,
    lp_ref,
    el_ref,
    diag,
    linv,
    ints,
    xs,
    st,
    tf,
    tp,
    tpt,
    fsc,
    lsc,
    picks,
    lpick,
    slab,
    mm,
    nn,
    kk,
    own,
    gg,
    hh,
    ff,
    bb,
    cc,
    rhs_s,
    send,
    recv,
    back,
    ret,
    dsem,
    ssem,
    rsem,
):
    reg = lax.axis_index("region")
    me = lax.axis_index("dom")

    bar = pltpu.get_barrier_semaphore()
    below, above = lax.rem(reg + groups - 1, groups), lax.rem(reg + 1, groups)

    def others(i):
        far = owners // 8
        dz = jnp.where(lax.rem(i, 2) == 1, far - (i + 1) // 2, far + i // 2)
        z = lax.rem(me // 4 + dz, owners // 4)
        return [z * 4 + lax.rem(me + dx, 4) for dx in (2, 1, 3, 0)]

    def greet(i, carry):
        for other in others(i):
            pl.semaphore_signal(bar, inc=1, device_id=(reg, other), device_id_type=MESH)
        return carry

    pl.semaphore_signal(bar, inc=1, device_id=(below, me), device_id_type=MESH)
    pl.semaphore_signal(bar, inc=1, device_id=(above, me), device_id_type=MESH)
    lax.fori_loop(0, owners // 4 - 1, greet, 0)
    for other in others(owners // 4 - 1)[:3]:
        pl.semaphore_signal(bar, inc=1, device_id=(reg, other), device_id_type=MESH)
    get_diag = pltpu.make_async_copy(diag_hbm, diag, dsem.at[0])
    get_linv = pltpu.make_async_copy(linv_hbm, linv, dsem.at[1])
    small = ((fs_hbm, fs_ref), (tmpl_hbm, tmpl_ref), (nb_hbm, nb_ref), (fp_hbm, fp_ref), (el_hbm, el_ref), (lp_hbm, lp_ref), (fsc_hbm, fsc_ref), (lsc_hbm, lsc_ref), (rs_hbm, rs_ref))
    fetches = [pltpu.make_async_copy(source, target, dsem.at[2 + i]) for i, (source, target) in enumerate(small)]
    for fetch in fetches:
        fetch.start()
    get_diag.start()
    get_linv.start()
    for fetch in fetches:
        fetch.wait()

    ints[...] = jnp.full((16, 128), -1.0, F32)
    ints[0:4, 0:ELEM] = nb_ref[...].astype(F32)
    ints[4:8, 0:ELEM] = fp_ref[...].astype(F32)
    ints[8:9, 0:ELEM] = el_ref[...].astype(F32)
    ints[9:11, 0:SLOTS] = lp_ref[...].astype(F32)
    columns = jnp.transpose(ints[...])

    xs[...] = jnp.zeros((EROWS, WIDE), F32)
    xs[0:ELEM, 0:BLOCK] = fs_ref[...]
    rounded = xs[...].astype(BF16)
    st[1] = rounded
    wide_state = rounded.astype(F32)

    tf[...] = jnp.zeros((TALL, WIDE), F32)
    for pattern in range(NPAT):
        tf[pattern * TSTEP : pattern * TSTEP + TRACE, 0:BLOCK] = tmpl_ref[pattern].astype(F32)
    tp[...] = tf[...].astype(BF16)
    tpt[...] = jnp.transpose(tf[...]).astype(BF16)
    fsc[...] = jnp.zeros((4, EROWS, WIDE), F32)
    for side in range(4):
        fsc[side, 0:ELEM, 0:BLOCK] = fsc_ref[:, side, :].astype(F32)
    lsc[...] = jnp.zeros((2, SLOTS, WIDE), F32)
    for side in range(2):
        lsc[side, :, 0:BLOCK] = lsc_ref[:, side, :].astype(F32)

    for side in range(4):
        picks[side] = picks_of(trace_column(OPPOSITE[side], TALL))
    lpick[...] = picks_of(jnp.where(lanes(1, 128) < TSTEP, trace_column(5, 128), trace_column(4, 128)))

    get_diag.wait()

    def own_rows_of(i, carry):
        for b in range(7):
            slab[i * 7 + b, 0:ELEM] = block_row(diag, ELEM, (i * 7 + b) * BLOCK)
        return carry

    lax.fori_loop(0, (BLOCK - 1) // 7, own_rows_of, 0)
    tail = diag[:, (BLOCK - 1) * BLOCK - 98 : BLOCK * BLOCK].astype(F32)
    slab[BLOCK - 1, 0:EROWS] = jnp.zeros((EROWS, WIDE), F32)
    slab[BLOCK - 1, 0:ELEM, 0:BLOCK] = tail[:, 98 : 98 + BLOCK]
    own[...] = jnp.zeros((EROWS, WIDE), F32)
    elem_lane = lanes(EROWS, WIDE)

    def own_rows(i, carry):
        total = own[...]
        for b in range(18):
            b = i * 18 + b
            total = jnp.where(elem_lane == b, lane_sums(slab[b, 0:EROWS] * wide_state), total)
        own[...] = total
        return carry

    lax.fori_loop(0, BLOCK // 18, own_rows, 0)

    get_linv.wait()

    def rows_of(i, carry):
        for b in range(7):
            slab[i * 7 + b] = block_row(linv, SLOTS, (i * 7 + b) * BLOCK)
        return carry

    lax.fori_loop(0, 12, rows_of, 0)

    pl.semaphore_wait(bar, owners + 1)
    up = pltpu.make_async_remote_copy(
        src_ref=st.at[1], dst_ref=st.at[0], send_sem=ssem.at[0], recv_sem=rsem.at[0], device_id=(above, me), device_id_type=MESH
    )
    down = pltpu.make_async_remote_copy(
        src_ref=st.at[1], dst_ref=st.at[2], send_sem=ssem.at[1], recv_sem=rsem.at[1], device_id=(below, me), device_id_type=MESH
    )
    up.start()
    down.start()
    lax.fori_loop(12, (BLOCK - 1) // 7, rows_of, 0)
    tail = linv[:, (BLOCK - 1) * BLOCK - 98 : BLOCK * BLOCK].astype(F32)
    slab[BLOCK - 1] = jnp.zeros((SLOTS, WIDE), F32)
    slab[BLOCK - 1, :, 0:BLOCK] = tail[:, 98 : 98 + BLOCK]
    up.wait()
    down.wait()

    stacked = jnp.concatenate([st[0], st[1], st[2]], axis=0)
    row_lane = lanes(EROWS, 3 * EROWS).astype(F32)
    has_below = jnp.where(reg > 0, 1.0, 0.0)
    has_above = jnp.where(reg < groups - 1, 1.0, 0.0)
    pieces = []
    for side in range(4):
        near = columns[0:EROWS, side : side + 1]
        part = jnp.where(near >= ELEM, 1.0, 0.0) + jnp.where(near >= 2 * ELEM, 1.0, 0.0)
        place = near + (EROWS - ELEM) * part
        present = jnp.where(part == 0.0, has_below, jnp.where(part == 2.0, has_above, 1.0))
        pick = jnp.where(row_lane == place, present, 0.0).astype(BF16)
        fetched = dot(pick, stacked).astype(BF16)
        spread = dot(fetched, picks[side])
        pattern = columns[0:EROWS, 4 + side : 5 + side]
        pieces.append(jnp.where((lanes(EROWS, TALL) // TSTEP).astype(F32) == pattern, spread, 0.0).astype(BF16))
    terms = dot(jnp.concatenate(pieces, axis=0), tp[...])
    total = own[...]
    for side in range(4):
        total = total + terms[side * EROWS : (side + 1) * EROWS] * fsc[side]
    xs[...] = jnp.zeros((EROWS, WIDE), F32)
    xs[0:ELEM, 0:BLOCK] = rs_ref[...]
    partial = xs[...] - total

    slot = columns[0:EROWS, 8:9]
    owner = jnp.floor(slot * (1.0 / SLOTS))
    local_slot = slot - owner * SLOTS
    traces = dot(rounded, lpick[...])
    traces = jnp.where(lanes(EROWS, 128) == 127, local_slot + 1.0, traces)
    owner_row = jnp.floor(ints[8:9, 0:EROWS] * (1.0 / SLOTS))
    pick_owner = jnp.where(lax.broadcasted_iota(jnp.int32, (owners, EROWS), 0).astype(F32) == owner_row, 1.0, 0.0)
    payload = jnp.concatenate([traces, partial], axis=1)
    send[:, 0, :] = dot(pick_owner, payload, precision=HIGHEST)

    def exchange(source, target, index):
        def one(other):
            pltpu.make_async_remote_copy(
                src_ref=source.at[other],
                dst_ref=target.at[me],
                send_sem=ssem.at[index],
                recv_sem=rsem.at[index],
                device_id=(reg, other),
                device_id_type=MESH,
            ).start()

        def four(i, carry):
            for other in others(i):
                one(other)
            return carry

        lax.fori_loop(0, owners // 4 - 1, four, 0)
        for other in others(owners // 4 - 1)[:3]:
            one(other)
        target[pl.ds(me, 1)] = source[pl.ds(me, 1)]

    def finish(source, target, index):
        whole = pltpu.make_async_remote_copy(
            src_ref=source.at[pl.ds(0, owners - 1)],
            dst_ref=target.at[pl.ds(0, owners - 1)],
            send_sem=ssem.at[index],
            recv_sem=rsem.at[index],
            device_id=(reg, lax.rem(me + 1, owners)),
            device_id_type=MESH,
        )
        whole.wait_send()
        whole.wait_recv()

    exchange(send, recv, 2)

    kinds = [columns[0:SLOTS, 9 + i : 10 + i] for i in range(2)]
    chosen = [jnp.where((lanes(SLOTS, TALL) // TSTEP).astype(F32) == kind, 1.0, 0.0) for kind in kinds]
    low_half = lanes(SLOTS, 128) < TSTEP

    def small_rows(i, carry):
        parts = []
        for u in range(3):
            first, last = slab[3 * (3 * i + u)], slab[3 * (3 * i + u) + 2]
            for x in (last * lsc[0], first * lsc[0], first * lsc[1]):
                parts.extend(halves(x))
        product = dot(jnp.concatenate(parts, axis=0), tpt[...])
        for u in range(3):
            m = 3 * i + u
            for n, (target, kind) in enumerate(((mm, 0), (kk, 0), (nn, 1))):
                at = (u * 6 + n * 2) * SLOTS
                x = (product[at : at + SLOTS] + product[at + SLOTS : at + 2 * SLOTS]) * chosen[kind]
                x = x[:, 0:128] + x[:, 128:256] + x[:, 256:384]
                x = jnp.where(low_half, x + pltpu.roll(x, TSTEP, 1), 0.0)
                if target is kk:
                    kk[m] = x
                else:
                    target[pl.ds(m, SLOTS, stride=MROWS), :] = x
        return carry

    lax.fori_loop(0, TRACE // 3, small_rows, 0)
    for m in range(TRACE, MROWS):
        mm[pl.ds(m, SLOTS, stride=MROWS), :] = jnp.zeros((SLOTS, 128), F32)
        nn[pl.ds(m, SLOTS, stride=MROWS), :] = jnp.zeros((SLOTS, 128), F32)

    finish(send, recv, 2)
    got = recv[:, 0, :]
    slot_column = got[:, 127:128] - 1.0
    to_slot = jnp.where(lanes(owners, SLOTS).astype(F32) == slot_column, 1.0, 0.0)
    from_source = jnp.transpose(to_slot)
    gathered = dot(from_source, got, precision=HIGHEST)
    filled = jnp.sum(from_source, axis=1, keepdims=True)
    place = lax.rem(lax.broadcasted_iota(jnp.int32, (SLOTS, 1), 0), LEN)
    lower = jnp.where(place > 0, filled, 0.0)
    upper = jnp.where(place < LEN - 1, pltpu.roll(jnp.broadcast_to(filled, (SLOTS, 128)), SLOTS - 1, 0)[:, 0:1], 0.0)

    def coupled(traces_before, traces_after):
        spreads = []
        for x, kind, gate in ((traces_before, 0, lower), (traces_after, 1, upper)):
            x = jnp.where(low_half & (gate > 0.5), x, 0.0)
            x = x + pltpu.roll(x, TSTEP, 1)
            spreads.append(jnp.concatenate([x, x, x], axis=1) * chosen[kind])
        x = jnp.concatenate(spreads, axis=0)
        high, low = halves(x)
        terms = dot(jnp.concatenate([high, low], axis=0), tp[...])
        terms = terms[0 : 2 * SLOTS] + terms[2 * SLOTS :]
        return terms[0:SLOTS] * lsc[0] + terms[SLOTS:] * lsc[1]

    line_traces = gathered[:, 0:128]
    tops = pltpu.roll(line_traces, 1, 0)
    bottoms = pltpu.roll(pltpu.roll(line_traces, TSTEP, 1), SLOTS - 1, 0)
    rhs = gathered[:, 128:384] - coupled(tops, bottoms)
    rhs_s[...] = rhs

    slot_lane = lanes(SLOTS, 128)
    gg[...] = jnp.zeros((SLOTS, 128), F32)
    hh[...] = jnp.zeros((SLOTS, 128), F32)

    def ends(i, carry):
        given, top, bottom = rhs_s[...], gg[...], hh[...]
        for m in range(9):
            m = i * 9 + m
            top = jnp.where(slot_lane == m, lane_sums(slab[3 * m + 2] * given), top)
            bottom = jnp.where(slot_lane == m, lane_sums(slab[3 * m] * given), bottom)
        gg[...] = top
        hh[...] = bottom
        return carry

    lax.fori_loop(0, TRACE // 9, ends, 0)

    eye = jnp.where(lanes(MROWS, 128) == lax.broadcasted_iota(jnp.int32, (MROWS, 128), 0), 1.0, 0.0)

    def sweep(matrices, given, out, reverse):
        def step(i, carry):
            position = LEN - 1 - i if reverse else i
            after = []
            for line in range(2):
                j = line * LEN + position
                matrix = matrices[pl.ds(pl.multiple_of(j * MROWS, 8), MROWS), :]
                column = jnp.sum(matrix * carry[line], axis=1, keepdims=True)
                row = given[pl.ds(j, 1), :] - jnp.sum(eye * column, axis=0, keepdims=True)
                out[pl.ds(j, 1), :] = row
                after.append(row)
            return tuple(after)

        zero = jnp.zeros((1, 128), F32)
        lax.fori_loop(0, LEN, step, (zero, zero))

    sweep(mm, gg, ff, False)
    before = jnp.where(lower > 0.5, pltpu.roll(ff[...], 1, 0), 0.0)
    ff[...] = before

    def reduce_first(i, carry):
        total, f = hh[...], ff[...]
        for m in range(18):
            m = i * 18 + m
            total = jnp.where(slot_lane == m, total - jnp.sum(kk[m] * f, axis=1, keepdims=True), total)
        hh[...] = total
        return carry

    lax.fori_loop(0, TRACE // 18, reduce_first, 0)
    hh[...] = jnp.where(filled > 0.5, hh[...], 0.0)
    sweep(nn, hh, bb, True)
    after = jnp.where(upper > 0.5, pltpu.roll(bb[...], SLOTS - 1, 0), 0.0)
    cc[...] = rhs_s[...] - coupled(before, after)

    send_lane = lanes(SLOTS, WIDE)
    ret[...] = jnp.zeros((SLOTS, WIDE), F32)

    def solve(i, carry):
        total, given = ret[...], cc[...]
        for b in range(18):
            b = i * 18 + b
            total = jnp.where(send_lane == b, lane_sums(slab[b] * given), total)
        ret[...] = total
        return carry

    lax.fori_loop(0, BLOCK // 18, solve, 0)
    both = jnp.concatenate([ret[...], rhs_s[...]], axis=1)
    answer = dot(to_slot, both, precision=HIGHEST)
    send[:, 0, :] = jnp.concatenate([answer[:, 0:128], answer[:, 256:384], jnp.where(slot_lane < TSTEP, answer[:, 128:256], pltpu.roll(answer[:, 384:512], TSTEP, 1))], axis=1)
    exchange(send, back, 3)
    finish(send, back, 3)
    answer = dot(jnp.transpose(pick_owner), back[:, 0, :], precision=HIGHEST)
    third = answer[:, 256:384]
    fixed = jnp.concatenate([answer[:, 0:128], third], axis=1)
    kept = jnp.concatenate([answer[:, 128:256], pltpu.roll(third, TSTEP, 1)], axis=1)
    ns_out[...] = fixed[0:ELEM, 0:BLOCK]
    res_out[...] = rs_ref[...] - kept[0:ELEM, 0:BLOCK]


def local(groups, owners, flow_state, right_side, diag_block, face_scale, face_pattern, neighbour, templates, line_inverse, line_scale, line_pattern, elem_line):
    operands = (
        flow_state,
        right_side,
        diag_block,
        face_scale,
        face_pattern.T,
        neighbour.T,
        jnp.transpose(templates, (1, 0, 2)),
        line_inverse,
        line_scale,
        line_pattern.T,
        elem_line[None, :],
    )
    vmem = pl.BlockSpec(memory_space=pltpu.VMEM)
    anywhere = pl.BlockSpec(memory_space=pl.ANY)
    message = pltpu.VMEM((owners, 1, MSG), F32)
    correction, removed = pl.pallas_call(
        functools.partial(kernel, groups, owners),
        out_shape=(jax.ShapeDtypeStruct((ELEM, BLOCK), F32), jax.ShapeDtypeStruct((ELEM, BLOCK), F32)),
        in_specs=[anywhere] * 11,
        out_specs=(vmem, vmem),
        scratch_shapes=[
            pltpu.VMEM((ELEM, BLOCK), F32),
            pltpu.VMEM((ELEM, BLOCK), F32),
            pltpu.VMEM((ELEM, 4, BLOCK), BF16),
            pltpu.VMEM((4, ELEM), jnp.int32),
            pltpu.VMEM((4, ELEM), jnp.int32),
            pltpu.VMEM((NPAT, TRACE, BLOCK), BF16),
            pltpu.VMEM((SLOTS, 2, BLOCK), BF16),
            pltpu.VMEM((2, SLOTS), jnp.int32),
            pltpu.VMEM((1, ELEM), jnp.int32),
            pltpu.VMEM((ELEM, BLOCK * BLOCK), BF16),
            pltpu.VMEM((SLOTS, BLOCK * BLOCK), BF16),
            pltpu.VMEM((16, 128), F32),
            pltpu.VMEM((EROWS, WIDE), F32),
            pltpu.VMEM((3, EROWS, WIDE), BF16),
            pltpu.VMEM((TALL, WIDE), F32),
            pltpu.VMEM((TALL, WIDE), BF16),
            pltpu.VMEM((WIDE, TALL), BF16),
            pltpu.VMEM((4, EROWS, WIDE), F32),
            pltpu.VMEM((2, SLOTS, WIDE), F32),
            pltpu.VMEM((4, WIDE, TALL), BF16),
            pltpu.VMEM((WIDE, 128), BF16),
            pltpu.VMEM((BLOCK, SLOTS, WIDE), F32),
            pltpu.VMEM((SLOTS * MROWS, 128), F32),
            pltpu.VMEM((SLOTS * MROWS, 128), F32),
            pltpu.VMEM((TRACE, SLOTS, 128), F32),
            pltpu.VMEM((EROWS, WIDE), F32),
            pltpu.VMEM((SLOTS, 128), F32),
            pltpu.VMEM((SLOTS, 128), F32),
            pltpu.VMEM((SLOTS, 128), F32),
            pltpu.VMEM((SLOTS, 128), F32),
            pltpu.VMEM((SLOTS, WIDE), F32),
            pltpu.VMEM((SLOTS, WIDE), F32),
            message,
            message,
            message,
            pltpu.VMEM((SLOTS, WIDE), F32),
            pltpu.SemaphoreType.DMA((2 + 9,)),
            pltpu.SemaphoreType.DMA((4,)),
            pltpu.SemaphoreType.DMA((4,)),
        ],
        compiler_params=pltpu.CompilerParams(collective_id=0, has_side_effects=True, vmem_limit_bytes=56 * 1024 * 1024),
    )(*operands)
    return flow_state + correction, right_side - removed


def solution(mesh):
    both = ("region", "dom")
    return jax.shard_map(
        functools.partial(local, mesh.shape["region"], mesh.shape["dom"]),
        mesh=mesh,
        in_specs=(
            P(both, None),
            P(both, None),
            P(both, None),
            P(both, None, None),
            P(both, None),
            P(both, None),
            P(),
            P(both, None),
            P(both, None, None),
            P(both, None),
            P(both),
        ),
        out_specs=(P(both, None), P(both, None)),
        check_vma=False,
    )
```

```python
import functools

import jax
import jax.numpy as jnp
import numpy as np
from jax import lax
from jax.experimental import pallas as pl
from jax.experimental.pallas import tpu as pltpu
from jax.sharding import PartitionSpec as P

MESH = pl.DeviceIdType.MESH
F32, BF16 = jnp.float32, jnp.bfloat16
OPPOSITE = (1, 0, 3, 2)

NV = 6
NPAT = 6
LEN = 32
BLOCK = 162
TRACE = 54
ELEM = 26
SLOTS = 64
EROWS = 32
WIDE = 256
TSTEP = 64
TALL = NPAT * TSTEP
MROWS = 56
MSG = 384


def trace_column(face_id, width):
    k = lax.rem(lanes(1, width), TSTEP).astype(F32)
    variable, rest = jnp.floor((k + 0.5) * (1.0 / 9.0)), 0.0
    line = jnp.floor((k + 0.5) * (1.0 / 3.0))
    if face_id < 2:
        rest = k + 18.0 * variable + 18.0 * face_id
    elif face_id < 4:
        rest = k + 6.0 * line + 6.0 * (face_id - 2)
    else:
        rest = 3.0 * k + 2.0 * (face_id - 4)
    return jnp.where(k < TRACE, rest, -1.0)


def picks_of(column):
    rows = lax.broadcasted_iota(jnp.int32, (WIDE, column.shape[1]), 0).astype(F32)
    return jnp.where(rows == column, 1.0, 0.0).astype(BF16)


def dot(a, b):
    return jnp.dot(a, b, preferred_element_type=F32)


def lanes(rows, width):
    return lax.broadcasted_iota(jnp.int32, (rows, width), 1)


def pick_rows(pick, x):
    pick = pick.astype(BF16)
    return dot(jnp.concatenate([pick, pick], axis=1), jnp.concatenate(halves(x), axis=0))


def halves(x):
    high = x.astype(BF16)
    return high, (x - high.astype(F32)).astype(BF16)


def block_row(ref, rows, start):
    base = pl.multiple_of((start // 128) * 128, 128)
    shift = lax.rem(128 - (start - base), 128)
    tiles = [ref[0:rows, pl.ds(pl.multiple_of(base + 128 * t, 128), 128)].astype(F32) for t in range(3)]
    moved = [pltpu.roll(tile, shift, 1) for tile in tiles]
    keep = lanes(rows, 128) < 128 - (start - base)
    return jnp.concatenate([jnp.where(keep, moved[0], moved[1]), jnp.where(keep, moved[1], moved[2])], axis=1)


def lane_sums(product):
    return jnp.sum(product[:, 0:128] + product[:, 128:256], axis=1, keepdims=True)


def kernel(
    groups,
    owners,
    fs_hbm,
    rs_hbm,
    diag_hbm,
    fsc_hbm,
    fp_hbm,
    nb_hbm,
    tmpl_hbm,
    linv_hbm,
    lsc_hbm,
    lp_hbm,
    el_hbm,
    out,
    fs_ref,
    rs_ref,
    fsc_ref,
    fp_ref,
    nb_ref,
    tmpl_ref,
    lsc_ref,
    lp_ref,
    el_ref,
    diag,
    linv,
    ints,
    xs,
    st,
    tf,
    tp,
    tp2,
    tpt,
    fsc,
    lsc,
    picks,
    lpick,
    slab,
    mm,
    nn,
    own,
    gcol,
    rows_p,
    gate_p,
    out_p,
    cc,
    rhs_s,
    send,
    recv,
    back,
    ret,
    dsem,
    ssem,
    rsem,
):
    reg = lax.axis_index("region")
    me = lax.axis_index("dom")

    bar = pltpu.get_barrier_semaphore()
    below, above = lax.rem(reg + groups - 1, groups), lax.rem(reg + 1, groups)

    def others(i):
        far = owners // 8
        dz = jnp.where(lax.rem(i, 2) == 1, far - (i + 1) // 2, far + i // 2)
        z = lax.rem(me // 4 + dz, owners // 4)
        return [z * 4 + lax.rem(me + dx, 4) for dx in (2, 1, 3, 0)]

    def greet(i, carry):
        for other in others(i):
            pl.semaphore_signal(bar, inc=1, device_id=(reg, other), device_id_type=MESH)
        return carry

    pl.semaphore_signal(bar, inc=1, device_id=(below, me), device_id_type=MESH)
    pl.semaphore_signal(bar, inc=1, device_id=(above, me), device_id_type=MESH)
    lax.fori_loop(0, owners // 4 - 1, greet, 0)
    for other in others(owners // 4 - 1)[:3]:
        pl.semaphore_signal(bar, inc=1, device_id=(reg, other), device_id_type=MESH)
    get_diag = pltpu.make_async_copy(diag_hbm, diag, dsem.at[0])
    get_linv = pltpu.make_async_copy(linv_hbm, linv, dsem.at[1])
    small = ((fs_hbm, fs_ref), (tmpl_hbm, tmpl_ref), (nb_hbm, nb_ref), (fp_hbm, fp_ref), (el_hbm, el_ref), (lp_hbm, lp_ref), (fsc_hbm, fsc_ref), (lsc_hbm, lsc_ref), (rs_hbm, rs_ref))
    fetches = [pltpu.make_async_copy(source, target, dsem.at[2 + i]) for i, (source, target) in enumerate(small)]
    for fetch in fetches:
        fetch.start()
    get_diag.start()
    get_linv.start()
    for fetch in fetches:
        fetch.wait()

    ints[...] = jnp.full((16, 128), -1.0, F32)
    ints[0:4, 0:ELEM] = nb_ref[...].astype(F32)
    ints[4:8, 0:ELEM] = fp_ref[...].astype(F32)
    ints[8:9, 0:ELEM] = el_ref[...].astype(F32)
    ints[9:11, 0:SLOTS] = lp_ref[...].astype(F32)
    columns = jnp.transpose(ints[...])

    xs[...] = jnp.zeros((EROWS, WIDE), F32)
    xs[0:ELEM, 0:BLOCK] = fs_ref[...]
    rounded = xs[...].astype(BF16)
    st[1] = rounded
    wide_state = rounded.astype(F32)

    tf[...] = jnp.zeros((TALL, WIDE), F32)
    for pattern in range(NPAT):
        tf[pattern * TSTEP : pattern * TSTEP + TRACE, 0:BLOCK] = tmpl_ref[pattern].astype(F32)
    tp[...] = tf[...].astype(BF16)
    turned = jnp.transpose(tf[...]).astype(BF16)
    tp2[0:TALL] = tp[...]
    tp2[TALL:] = tp[...]
    tpt[0:WIDE] = turned
    tpt[WIDE:] = turned
    fsc[...] = jnp.zeros((4, EROWS, WIDE), F32)
    for side in range(4):
        fsc[side, 0:ELEM, 0:BLOCK] = fsc_ref[:, side, :].astype(F32)
    lsc[...] = jnp.zeros((2, SLOTS, WIDE), F32)
    for side in range(2):
        lsc[side, :, 0:BLOCK] = lsc_ref[:, side, :].astype(F32)

    for side in range(4):
        picks[side] = picks_of(trace_column(OPPOSITE[side], TALL))
    lpick[...] = picks_of(jnp.where(lanes(1, 128) < TSTEP, trace_column(5, 128), trace_column(4, 128)))

    get_diag.wait()

    def own_rows_of(i, carry):
        for b in range(23):
            slab[i * 23 + b, 0:ELEM] = block_row(diag, ELEM, (i * 23 + b) * BLOCK)
        return carry

    lax.fori_loop(0, (BLOCK - 1) // 23, own_rows_of, 0)
    tail = diag[:, (BLOCK - 1) * BLOCK - 98 : BLOCK * BLOCK].astype(F32)
    slab[BLOCK - 1, 0:EROWS] = jnp.zeros((EROWS, WIDE), F32)
    slab[BLOCK - 1, 0:ELEM, 0:BLOCK] = tail[:, 98 : 98 + BLOCK]
    own[...] = jnp.zeros((EROWS, WIDE), F32)
    elem_lane = lanes(EROWS, WIDE)

    def own_rows(i, carry):
        total = own[...]
        for b in range(54):
            b = i * 54 + b
            total = jnp.where(elem_lane == b, lane_sums(slab[b, 0:EROWS] * wide_state), total)
        own[...] = total
        return carry

    lax.fori_loop(0, BLOCK // 54, own_rows, 0)

    get_linv.wait()

    def rows_of(i, carry):
        for b in range(23):
            slab[i * 23 + b] = block_row(linv, SLOTS, (i * 23 + b) * BLOCK)
        return carry

    lax.fori_loop(0, 4, rows_of, 0)

    pl.semaphore_wait(bar, owners + 1)
    up = pltpu.make_async_remote_copy(
        src_ref=st.at[1], dst_ref=st.at[0], send_sem=ssem.at[0], recv_sem=rsem.at[0], device_id=(above, me), device_id_type=MESH
    )
    down = pltpu.make_async_remote_copy(
        src_ref=st.at[1], dst_ref=st.at[2], send_sem=ssem.at[1], recv_sem=rsem.at[1], device_id=(below, me), device_id_type=MESH
    )
    up.start()
    down.start()
    lax.fori_loop(4, (BLOCK - 1) // 23, rows_of, 0)
    tail = linv[:, (BLOCK - 1) * BLOCK - 98 : BLOCK * BLOCK].astype(F32)
    slab[BLOCK - 1] = jnp.zeros((SLOTS, WIDE), F32)
    slab[BLOCK - 1, :, 0:BLOCK] = tail[:, 98 : 98 + BLOCK]
    up.wait()
    down.wait()

    stacked = jnp.concatenate([st[0], st[1], st[2]], axis=0)
    row_lane = lanes(EROWS, 3 * EROWS).astype(F32)
    has_below = jnp.where(reg > 0, 1.0, 0.0)
    has_above = jnp.where(reg < groups - 1, 1.0, 0.0)
    pieces = []
    for side in range(4):
        near = columns[0:EROWS, side : side + 1]
        part = jnp.where(near >= ELEM, 1.0, 0.0) + jnp.where(near >= 2 * ELEM, 1.0, 0.0)
        place = near + (EROWS - ELEM) * part
        present = jnp.where(part == 0.0, has_below, jnp.where(part == 2.0, has_above, 1.0))
        pick = jnp.where(row_lane == place, present, 0.0).astype(BF16)
        fetched = dot(pick, stacked).astype(BF16)
        spread = dot(fetched, picks[side])
        pattern = columns[0:EROWS, 4 + side : 5 + side]
        pieces.append(jnp.where((lanes(EROWS, TALL) // TSTEP).astype(F32) == pattern, spread, 0.0).astype(BF16))
    terms = dot(jnp.concatenate(pieces, axis=0), tp[...])
    total = own[...]
    for side in range(4):
        total = total + terms[side * EROWS : (side + 1) * EROWS] * fsc[side]
    xs[...] = jnp.zeros((EROWS, WIDE), F32)
    xs[0:ELEM, 0:BLOCK] = rs_ref[...]
    partial = xs[...] - total

    slot = columns[0:EROWS, 8:9]
    owner = jnp.floor(slot * (1.0 / SLOTS))
    local_slot = slot - owner * SLOTS
    traces = dot(rounded, lpick[...])
    traces = jnp.where(lanes(EROWS, 128) == 127, local_slot + 1.0, traces)
    owner_row = jnp.floor(ints[8:9, 0:EROWS] * (1.0 / SLOTS))
    pick_owner = jnp.where(lax.broadcasted_iota(jnp.int32, (owners, EROWS), 0).astype(F32) == owner_row, 1.0, 0.0)
    payload = jnp.concatenate([traces, partial], axis=1)
    send[:, 0, :] = pick_rows(pick_owner, payload)

    def exchange(source, target, index):
        def one(other):
            pltpu.make_async_remote_copy(
                src_ref=source.at[other],
                dst_ref=target.at[me],
                send_sem=ssem.at[index],
                recv_sem=rsem.at[index],
                device_id=(reg, other),
                device_id_type=MESH,
            ).start()

        def four(i, carry):
            for other in others(i):
                one(other)
            return carry

        lax.fori_loop(0, owners // 4 - 1, four, 0)
        for other in others(owners // 4 - 1)[:3]:
            one(other)
        target[pl.ds(me, 1)] = source[pl.ds(me, 1)]

    def finish(source, target, index):
        whole = pltpu.make_async_remote_copy(
            src_ref=source.at[pl.ds(0, owners - 1)],
            dst_ref=target.at[pl.ds(0, owners - 1)],
            send_sem=ssem.at[index],
            recv_sem=rsem.at[index],
            device_id=(reg, lax.rem(me + 1, owners)),
            device_id_type=MESH,
        )
        whole.wait_send()
        whole.wait_recv()

    exchange(send, recv, 2)

    kinds = [columns[0:SLOTS, 9 + i : 10 + i] for i in range(2)]
    chosen = [jnp.where((lanes(SLOTS, TALL) // TSTEP).astype(F32) == kind, 1.0, 0.0) for kind in kinds]
    low_half = lanes(SLOTS, 128) < TSTEP
    own_half = lanes(SLOTS, 128) // TSTEP == lax.broadcasted_iota(jnp.int32, (SLOTS, 128), 0) // LEN

    def store_rows(target, m, x):
        target[pl.ds(m, LEN, stride=2 * TSTEP), :] = x[0:LEN]
        target[pl.ds(m + TSTEP, LEN, stride=2 * TSTEP), :] = x[LEN:]

    def small_rows(i, carry):
        parts = []
        for u in range(9):
            m = 9 * i + u
            for x in (slab[3 * m + 2] * lsc[0], slab[3 * m] * lsc[1]):
                parts.append(jnp.concatenate(halves(x), axis=1))
        product = dot(jnp.concatenate(parts, axis=0), tpt[...])
        for u in range(9):
            for kind, target in enumerate((mm, nn)):
                at = (u * 2 + kind) * SLOTS
                x = product[at : at + SLOTS] * chosen[kind]
                x = x[:, 0:128] + x[:, 128:256] + x[:, 256:384]
                x = x + pltpu.roll(x, TSTEP, 1)
                store_rows(target, 9 * i + u, jnp.where(own_half, x, 0.0))
        return carry

    lax.fori_loop(0, TRACE // 9, small_rows, 0)
    for m in range(TRACE, TSTEP):
        for target in (mm, nn, gcol):
            store_rows(target, m, jnp.zeros((SLOTS, 128), F32))

    def turn(i, carry):
        for target, position in ((mm, 2 * i + 1), (nn, 2 * i)):
            at = pl.multiple_of(position * 2 * TSTEP, 128)
            block = target[pl.ds(at, TSTEP), :] + target[pl.ds(at + TSTEP, TSTEP), :]
            block = jnp.transpose(block)
            target[pl.ds(at, TSTEP), :] = jnp.concatenate([block[0:TSTEP], block[TSTEP:]], axis=1)
        return carry

    lax.fori_loop(0, LEN // 2, turn, 0, unroll=8)

    finish(send, recv, 2)
    got = recv[:, 0, :]
    slot_column = got[:, 127:128] - 1.0
    to_slot = jnp.where(lanes(owners, SLOTS).astype(F32) == slot_column, 1.0, 0.0)
    from_source = jnp.transpose(to_slot)
    gathered = pick_rows(from_source, got)
    filled = jnp.sum(from_source, axis=1, keepdims=True)
    place = lax.rem(lax.broadcasted_iota(jnp.int32, (SLOTS, 1), 0), LEN)
    lower = jnp.where(place > 0, filled, 0.0)
    upper = jnp.where(place < LEN - 1, pltpu.roll(jnp.broadcast_to(filled, (SLOTS, 128)), SLOTS - 1, 0)[:, 0:1], 0.0)

    def coupled(kind, gate, x):
        x = jnp.where(gate > 0.5, x, 0.0)
        spread = jnp.concatenate([x, x, x], axis=1) * chosen[kind]
        return dot(jnp.concatenate(halves(spread), axis=1), tp2[...]) * lsc[kind]

    line_traces = gathered[:, 0:128]
    swapped = pltpu.roll(line_traces, TSTEP, 1)
    tops = jnp.where(low_half, line_traces, swapped)
    bottoms = jnp.where(low_half, swapped, line_traces)
    rhs = gathered[:, 128:384] - coupled(0, lower, pltpu.roll(tops, 1, 0)) - coupled(1, upper, pltpu.roll(bottoms, SLOTS - 1, 0))
    rhs_s[...] = rhs

    slot_lane = lanes(SLOTS, 128)
    row_lane = lanes(LEN, 128)

    def trace_of_solution(given, first, gate):
        x, rows = given[...], jnp.zeros((LEN, 128), F32)
        for m in range(TRACE):
            value = jnp.broadcast_to(lane_sums(slab[3 * m + first] * x), (SLOTS, 128))
            if gate is not None:
                value = jnp.where(gate > 0.5, value, 0.0)
            store_rows(gcol, m, value)
            rows = jnp.where(row_lane == m, value[0:LEN], jnp.where(row_lane == m + TSTEP, value[LEN:], rows))
        rows_p[...] = jnp.broadcast_to(rows[:, None, :], (LEN, 8, 128))

    gates = jnp.where(row_lane < TSTEP, filled[0:LEN], filled[LEN:])
    gate_p[...] = jnp.broadcast_to(gates[:, None, :], (LEN, 8, 128))
    trace_of_solution(rhs_s, 2, None)

    tiles = MROWS // 8
    place8 = [lax.broadcasted_iota(jnp.int32, (tiles, 8, 128), i) for i in range(3)]
    eye = jnp.where(place8[2] % TSTEP == 8 * place8[0] + place8[1], 1.0, 0.0)
    first_line = place8[2] < TSTEP

    def sweep(matrices, reverse):
        def pair(i, row):
            first = LEN - 1 - 2 * i if reverse else 2 * i
            second = first - 1 if reverse else first + 1
            at = pl.multiple_of(first * 2 * TSTEP, 128)
            column = []
            for line in range(2):
                block = pl.ds(at + line * TSTEP, MROWS)
                product = matrices[block, :].reshape(tiles, 8, 128) * row[None]
                column.append(gcol[block, :].reshape(tiles, 8, 128) - jnp.sum(product, axis=2, keepdims=True))
            column = jnp.where(first_line, column[0], column[1])
            out_p[pl.ds(first, 1), :] = jnp.sum(jnp.sum(eye * column, axis=0), axis=0, keepdims=True)
            turned = matrices[pl.ds(pl.multiple_of(second * 2 * TSTEP, 128), MROWS), :].reshape(tiles, 8, 128)
            moved = jnp.sum(jnp.sum(turned * column, axis=0), axis=0, keepdims=True)
            row = jnp.where(gate_p[second] > 0.5, rows_p[second] - moved, 0.0)
            out_p[pl.ds(second, 1), :] = row[0:1]
            return row

        lax.fori_loop(0, LEN // 2, pair, jnp.zeros((8, 128), F32), unroll=8)
        x = out_p[...]
        swapped = pltpu.roll(x, TSTEP, 1)
        low = row_lane < TSTEP
        return jnp.concatenate([jnp.where(low, x, swapped), jnp.where(low, swapped, x)], axis=0)

    forward = sweep(mm, False)

    cc[...] = rhs_s[...] - coupled(0, lower, pltpu.roll(forward, 1, 0))
    trace_of_solution(cc, 0, filled)

    backward = sweep(nn, True)

    cc[...] = cc[...] - coupled(1, upper, pltpu.roll(backward, SLOTS - 1, 0))

    send_lane = lanes(SLOTS, WIDE)
    ret[...] = jnp.zeros((SLOTS, WIDE), F32)

    def solve(i, carry):
        total, given = ret[...], cc[...]
        for b in range(54):
            b = i * 54 + b
            total = jnp.where(send_lane == b, lane_sums(slab[b] * given), total)
        ret[...] = total
        return carry

    lax.fori_loop(0, BLOCK // 54, solve, 0)
    both = jnp.concatenate([ret[...], rhs_s[...]], axis=1)
    answer = pick_rows(to_slot, both)
    send[:, 0, :] = jnp.concatenate([answer[:, 0:128], answer[:, 256:384], jnp.where(slot_lane < TSTEP, answer[:, 128:256], pltpu.roll(answer[:, 384:512], TSTEP, 1))], axis=1)
    exchange(send, back, 3)
    finish(send, back, 3)
    answer = pick_rows(jnp.transpose(pick_owner), back[:, 0, :])
    third = answer[:, 256:384]
    fixed = jnp.concatenate([answer[:, 0:128], third], axis=1)
    kept = jnp.concatenate([answer[:, 128:256], pltpu.roll(third, TSTEP, 1)], axis=1)
    out[0] = fixed[0:ELEM, 0:BLOCK]
    out[1] = rs_ref[...] - kept[0:ELEM, 0:BLOCK]


def local(groups, owners, flow_state, right_side, diag_block, face_scale, face_pattern, neighbour, templates, line_inverse, line_scale, line_pattern, elem_line):
    operands = (
        flow_state,
        right_side,
        diag_block,
        face_scale,
        face_pattern.T,
        neighbour.T,
        jnp.transpose(templates, (1, 0, 2)),
        line_inverse,
        line_scale,
        line_pattern.T,
        elem_line[None, :],
    )
    vmem = pl.BlockSpec(memory_space=pltpu.VMEM)
    anywhere = pl.BlockSpec(memory_space=pl.ANY)
    message = pltpu.VMEM((owners, 1, MSG), F32)
    both = pl.pallas_call(
        functools.partial(kernel, groups, owners),
        out_shape=jax.ShapeDtypeStruct((2, ELEM, BLOCK), F32),
        in_specs=[anywhere] * 11,
        out_specs=vmem,
        scratch_shapes=[
            pltpu.VMEM((ELEM, BLOCK), F32),
            pltpu.VMEM((ELEM, BLOCK), F32),
            pltpu.VMEM((ELEM, 4, BLOCK), BF16),
            pltpu.VMEM((4, ELEM), jnp.int32),
            pltpu.VMEM((4, ELEM), jnp.int32),
            pltpu.VMEM((NPAT, TRACE, BLOCK), BF16),
            pltpu.VMEM((SLOTS, 2, BLOCK), BF16),
            pltpu.VMEM((2, SLOTS), jnp.int32),
            pltpu.VMEM((1, ELEM), jnp.int32),
            pltpu.VMEM((ELEM, BLOCK * BLOCK), BF16),
            pltpu.VMEM((SLOTS, BLOCK * BLOCK), BF16),
            pltpu.VMEM((16, 128), F32),
            pltpu.VMEM((EROWS, WIDE), F32),
            pltpu.VMEM((3, EROWS, WIDE), BF16),
            pltpu.VMEM((TALL, WIDE), F32),
            pltpu.VMEM((TALL, WIDE), BF16),
            pltpu.VMEM((2 * TALL, WIDE), BF16),
            pltpu.VMEM((2 * WIDE, TALL), BF16),
            pltpu.VMEM((4, EROWS, WIDE), F32),
            pltpu.VMEM((2, SLOTS, WIDE), F32),
            pltpu.VMEM((4, WIDE, TALL), BF16),
            pltpu.VMEM((WIDE, 128), BF16),
            pltpu.VMEM((BLOCK, SLOTS, WIDE), F32),
            pltpu.VMEM((SLOTS * TSTEP, 128), F32),
            pltpu.VMEM((SLOTS * TSTEP, 128), F32),
            pltpu.VMEM((EROWS, WIDE), F32),
            pltpu.VMEM((SLOTS * TSTEP, 128), F32),
            pltpu.VMEM((LEN, 8, 128), F32),
            pltpu.VMEM((LEN, 8, 128), F32),
            pltpu.VMEM((LEN, 128), F32),
            pltpu.VMEM((SLOTS, WIDE), F32),
            pltpu.VMEM((SLOTS, WIDE), F32),
            message,
            message,
            message,
            pltpu.VMEM((SLOTS, WIDE), F32),
            pltpu.SemaphoreType.DMA((2 + 9,)),
            pltpu.SemaphoreType.DMA((4,)),
            pltpu.SemaphoreType.DMA((4,)),
        ],
        compiler_params=pltpu.CompilerParams(collective_id=0, has_side_effects=True, vmem_limit_bytes=56 * 1024 * 1024),
    )(*operands)
    return flow_state + both[0], right_side - both[1]


def solution(mesh):
    both = ("region", "dom")
    return jax.shard_map(
        functools.partial(local, mesh.shape["region"], mesh.shape["dom"]),
        mesh=mesh,
        in_specs=(
            P(both, None),
            P(both, None),
            P(both, None),
            P(both, None, None),
            P(both, None),
            P(both, None),
            P(),
            P(both, None),
            P(both, None, None),
            P(both, None),
            P(both),
        ),
        out_specs=(P(both, None), P(both, None)),
        check_vma=False,
    )
```

```python
import functools

import jax
import jax.numpy as jnp
import numpy as np
from jax import lax
from jax.experimental import pallas as pl
from jax.experimental.pallas import tpu as pltpu
from jax.sharding import PartitionSpec as P

MESH = pl.DeviceIdType.MESH
F32, BF16 = jnp.float32, jnp.bfloat16
OPPOSITE = (1, 0, 3, 2)

NV = 6
NPAT = 6
LEN = 32
BLOCK = 162
TRACE = 54
ELEM = 26
SLOTS = 64
EROWS = 32
WIDE = 256
TSTEP = 64
TALL = NPAT * TSTEP
MROWS = 56


def trace_column(face_id, width):
    k = lax.rem(lanes(1, width), TSTEP).astype(F32)
    variable, rest = jnp.floor((k + 0.5) * (1.0 / 9.0)), 0.0
    line = jnp.floor((k + 0.5) * (1.0 / 3.0))
    if face_id < 2:
        rest = k + 18.0 * variable + 18.0 * face_id
    elif face_id < 4:
        rest = k + 6.0 * line + 6.0 * (face_id - 2)
    else:
        rest = 3.0 * k + 2.0 * (face_id - 4)
    return jnp.where(k < TRACE, rest, -1.0)


def picks_of(column):
    rows = lax.broadcasted_iota(jnp.int32, (WIDE, column.shape[1]), 0).astype(F32)
    return jnp.where(rows == column, 1.0, 0.0).astype(BF16)


def dot(a, b):
    return jnp.dot(a, b, preferred_element_type=F32)


def lanes(rows, width):
    return lax.broadcasted_iota(jnp.int32, (rows, width), 1)


def pick_rows(pick, x):
    pick = pick.astype(BF16)
    return dot(jnp.concatenate([pick, pick], axis=1), jnp.concatenate(halves(x), axis=0))


def halves(x):
    high = x.astype(BF16)
    return high, (x - high.astype(F32)).astype(BF16)


def block_row(ref, rows, start):
    base = pl.multiple_of((start // 128) * 128, 128)
    shift = lax.rem(128 - (start - base), 128)
    tiles = [ref[0:rows, pl.ds(pl.multiple_of(base + 128 * t, 128), 128)].astype(F32) for t in range(3)]
    moved = [pltpu.roll(tile, shift, 1) for tile in tiles]
    keep = lanes(rows, 128) < 128 - (start - base)
    return jnp.concatenate([jnp.where(keep, moved[0], moved[1]), jnp.where(keep, moved[1], moved[2])], axis=1)


def lane_sums(product):
    return jnp.sum(product[:, 0:128] + product[:, 128:256], axis=1, keepdims=True)


def kernel(
    groups,
    owners,
    fs_hbm,
    rs_hbm,
    diag_hbm,
    fsc_hbm,
    fp_hbm,
    nb_hbm,
    tmpl_hbm,
    linv_hbm,
    lsc_hbm,
    lp_hbm,
    el_hbm,
    out,
    fs_ref,
    rs_ref,
    fsc_ref,
    fp_ref,
    nb_ref,
    tmpl_ref,
    lsc_ref,
    lp_ref,
    el_ref,
    diag,
    linv,
    ints,
    xs,
    st,
    tf,
    tp,
    tp2,
    tpt,
    fsc,
    lsc,
    picks,
    lpick,
    slab,
    mm,
    nn,
    own,
    gcol,
    rows_p,
    gate_p,
    out_p,
    cc,
    rhs_s,
    send_t,
    recv_t,
    send_p,
    recv_p,
    send_r,
    back_r,
    send_c,
    back_c,
    ret,
    dsem,
    ssem,
    rsem,
):
    reg = lax.axis_index("region")
    me = lax.axis_index("dom")

    bar = pltpu.get_barrier_semaphore()
    below, above = lax.rem(reg + groups - 1, groups), lax.rem(reg + 1, groups)

    def others(i):
        far = owners // 8
        dz = jnp.where(lax.rem(i, 2) == 1, far - (i + 1) // 2, far + i // 2)
        z = lax.rem(me // 4 + dz, owners // 4)
        return [z * 4 + lax.rem(me + dx, 4) for dx in (2, 1, 3, 0)]

    def greet(i, carry):
        for other in others(i):
            pl.semaphore_signal(bar, inc=1, device_id=(reg, other), device_id_type=MESH)
        return carry

    pl.semaphore_signal(bar, inc=1, device_id=(below, me), device_id_type=MESH)
    pl.semaphore_signal(bar, inc=1, device_id=(above, me), device_id_type=MESH)
    lax.fori_loop(0, owners // 4 - 1, greet, 0)
    for other in others(owners // 4 - 1)[:3]:
        pl.semaphore_signal(bar, inc=1, device_id=(reg, other), device_id_type=MESH)
    get_diag = pltpu.make_async_copy(diag_hbm, diag, dsem.at[0])
    get_linv = pltpu.make_async_copy(linv_hbm, linv, dsem.at[1])
    small = ((fs_hbm, fs_ref), (tmpl_hbm, tmpl_ref), (nb_hbm, nb_ref), (fp_hbm, fp_ref), (el_hbm, el_ref), (lp_hbm, lp_ref), (fsc_hbm, fsc_ref), (lsc_hbm, lsc_ref), (rs_hbm, rs_ref))
    fetches = [pltpu.make_async_copy(source, target, dsem.at[2 + i]) for i, (source, target) in enumerate(small)]
    for fetch in fetches:
        fetch.start()
    get_diag.start()
    get_linv.start()
    for fetch in fetches:
        fetch.wait()

    ints[...] = jnp.full((16, 128), -1.0, F32)
    ints[0:4, 0:ELEM] = nb_ref[...].astype(F32)
    ints[4:8, 0:ELEM] = fp_ref[...].astype(F32)
    ints[8:9, 0:ELEM] = el_ref[...].astype(F32)
    ints[9:11, 0:SLOTS] = lp_ref[...].astype(F32)
    columns = jnp.transpose(ints[...])

    xs[...] = jnp.zeros((EROWS, WIDE), F32)
    xs[0:ELEM, 0:BLOCK] = fs_ref[...]
    rounded = xs[...].astype(BF16)
    st[1] = rounded
    wide_state = rounded.astype(F32)

    tf[...] = jnp.zeros((TALL, WIDE), F32)
    for pattern in range(NPAT):
        tf[pattern * TSTEP : pattern * TSTEP + TRACE, 0:BLOCK] = tmpl_ref[pattern].astype(F32)
    tp[...] = tf[...].astype(BF16)
    turned = jnp.transpose(tf[...]).astype(BF16)
    tp2[0:TALL] = tp[...]
    tp2[TALL:] = tp[...]
    tpt[0:WIDE] = turned
    tpt[WIDE:] = turned
    fsc[...] = jnp.zeros((4, EROWS, WIDE), F32)
    for side in range(4):
        fsc[side, 0:ELEM, 0:BLOCK] = fsc_ref[:, side, :].astype(F32)
    lsc[...] = jnp.zeros((2, SLOTS, WIDE), F32)
    for side in range(2):
        lsc[side, :, 0:BLOCK] = lsc_ref[:, side, :].astype(F32)

    for side in range(4):
        picks[side] = picks_of(trace_column(OPPOSITE[side], TALL))
    lpick[...] = picks_of(jnp.where(lanes(1, 128) < TSTEP, trace_column(5, 128), trace_column(4, 128)))

    get_diag.wait()

    def own_rows_of(i, carry):
        for b in range(23):
            slab[i * 23 + b, 0:ELEM] = block_row(diag, ELEM, (i * 23 + b) * BLOCK)
        return carry

    lax.fori_loop(0, (BLOCK - 1) // 23, own_rows_of, 0)
    tail = diag[:, (BLOCK - 1) * BLOCK - 98 : BLOCK * BLOCK].astype(F32)
    slab[BLOCK - 1, 0:EROWS] = jnp.zeros((EROWS, WIDE), F32)
    slab[BLOCK - 1, 0:ELEM, 0:BLOCK] = tail[:, 98 : 98 + BLOCK]
    own[...] = jnp.zeros((EROWS, WIDE), F32)
    elem_lane = lanes(EROWS, WIDE)

    def own_rows(i, carry):
        total = own[...]
        for b in range(54):
            b = i * 54 + b
            total = jnp.where(elem_lane == b, lane_sums(slab[b, 0:EROWS] * wide_state), total)
        own[...] = total
        return carry

    lax.fori_loop(0, BLOCK // 54, own_rows, 0)

    get_linv.wait()

    def rows_of(i, carry):
        for b in range(23):
            slab[i * 23 + b] = block_row(linv, SLOTS, (i * 23 + b) * BLOCK)
        return carry

    lax.fori_loop(0, (BLOCK - 1) // 23, rows_of, 0)
    tail = linv[:, (BLOCK - 1) * BLOCK - 98 : BLOCK * BLOCK].astype(F32)
    slab[BLOCK - 1] = jnp.zeros((SLOTS, WIDE), F32)
    slab[BLOCK - 1, :, 0:BLOCK] = tail[:, 98 : 98 + BLOCK]

    slot = columns[0:EROWS, 8:9]
    local_slot = slot - jnp.floor(slot * (1.0 / SLOTS)) * SLOTS
    traces = dot(rounded, lpick[...])
    traces = jnp.where(lanes(EROWS, 128) == 127, local_slot + 1.0, traces)
    owner_row = jnp.floor(ints[8:9, 0:EROWS] * (1.0 / SLOTS))
    pick_owner = jnp.where(lax.broadcasted_iota(jnp.int32, (owners, EROWS), 0).astype(F32) == owner_row, 1.0, 0.0)
    send_t[:, 0, :] = dot(pick_owner.astype(BF16), traces.astype(BF16))

    def send_one(source, target, index, other):
        pltpu.make_async_remote_copy(
            src_ref=source.at[other],
            dst_ref=target.at[me],
            send_sem=ssem.at[index],
            recv_sem=rsem.at[index],
            device_id=(reg, other),
            device_id_type=MESH,
        ).start()

    def exchange(source, target, index):
        def four(i, carry):
            for other in others(i):
                send_one(source, target, index, other)
            return carry

        lax.fori_loop(0, owners // 4 - 1, four, 0)
        for other in others(owners // 4 - 1)[:3]:
            send_one(source, target, index, other)
        target[pl.ds(me, 1)] = source[pl.ds(me, 1)]

    def finish(source, target, index):
        whole = pltpu.make_async_remote_copy(
            src_ref=source.at[pl.ds(0, owners - 1)],
            dst_ref=target.at[pl.ds(0, owners - 1)],
            send_sem=ssem.at[index],
            recv_sem=rsem.at[index],
            device_id=(reg, lax.rem(me + 1, owners)),
            device_id_type=MESH,
        )
        whole.wait_send()
        whole.wait_recv()

    kinds = [columns[0:SLOTS, 9 + i : 10 + i] for i in range(2)]
    chosen = [jnp.where((lanes(SLOTS, TALL) // TSTEP).astype(F32) == kind, 1.0, 0.0) for kind in kinds]
    low_half = lanes(SLOTS, 128) < TSTEP
    own_half = lanes(SLOTS, 128) // TSTEP == lax.broadcasted_iota(jnp.int32, (SLOTS, 128), 0) // LEN

    def store_rows(target, m, x):
        target[pl.ds(m, LEN, stride=2 * TSTEP), :] = x[0:LEN]
        target[pl.ds(m + TSTEP, LEN, stride=2 * TSTEP), :] = x[LEN:]

    def small_rows(i, carry):
        parts = []
        for u in range(9):
            m = 9 * i + u
            for x in (slab[3 * m + 2] * lsc[0], slab[3 * m] * lsc[1]):
                parts.append(jnp.concatenate(halves(x), axis=1))
        product = dot(jnp.concatenate(parts, axis=0), tpt[...])
        for u in range(9):
            for kind, target in enumerate((mm, nn)):
                at = (u * 2 + kind) * SLOTS
                x = product[at : at + SLOTS] * chosen[kind]
                x = x[:, 0:128] + x[:, 128:256] + x[:, 256:384]
                x = x + pltpu.roll(x, TSTEP, 1)
                store_rows(target, 9 * i + u, jnp.where(own_half, x, 0.0))
        return carry

    pl.semaphore_wait(bar, owners + 1)
    up = pltpu.make_async_remote_copy(
        src_ref=st.at[1], dst_ref=st.at[0], send_sem=ssem.at[0], recv_sem=rsem.at[0], device_id=(above, me), device_id_type=MESH
    )
    down = pltpu.make_async_remote_copy(
        src_ref=st.at[1], dst_ref=st.at[2], send_sem=ssem.at[1], recv_sem=rsem.at[1], device_id=(below, me), device_id_type=MESH
    )
    up.start()
    down.start()
    exchange(send_t, recv_t, 2)
    lax.fori_loop(0, 3, small_rows, 0)
    up.wait()
    down.wait()

    stacked = jnp.concatenate([st[0], st[1], st[2]], axis=0)
    row_lane = lanes(EROWS, 3 * EROWS).astype(F32)
    has_below = jnp.where(reg > 0, 1.0, 0.0)
    has_above = jnp.where(reg < groups - 1, 1.0, 0.0)
    pieces = []
    for side in range(4):
        near = columns[0:EROWS, side : side + 1]
        part = jnp.where(near >= ELEM, 1.0, 0.0) + jnp.where(near >= 2 * ELEM, 1.0, 0.0)
        place = near + (EROWS - ELEM) * part
        present = jnp.where(part == 0.0, has_below, jnp.where(part == 2.0, has_above, 1.0))
        pick = jnp.where(row_lane == place, present, 0.0).astype(BF16)
        fetched = dot(pick, stacked).astype(BF16)
        spread = dot(fetched, picks[side])
        pattern = columns[0:EROWS, 4 + side : 5 + side]
        pieces.append(jnp.where((lanes(EROWS, TALL) // TSTEP).astype(F32) == pattern, spread, 0.0).astype(BF16))
    terms = dot(jnp.concatenate(pieces, axis=0), tp[...])
    total = own[...]
    for side in range(4):
        total = total + terms[side * EROWS : (side + 1) * EROWS] * fsc[side]
    xs[...] = jnp.zeros((EROWS, WIDE), F32)
    xs[0:ELEM, 0:BLOCK] = rs_ref[...]
    send_p[:, 0, :] = pick_rows(pick_owner, xs[...] - total)
    exchange(send_p, recv_p, 3)

    lax.fori_loop(3, TRACE // 9, small_rows, 0)
    for m in range(TRACE, TSTEP):
        for target in (mm, nn, gcol):
            store_rows(target, m, jnp.zeros((SLOTS, 128), F32))

    def turn(i, carry):
        for target, position in ((mm, 2 * i + 1), (nn, 2 * i)):
            at = pl.multiple_of(position * 2 * TSTEP, 128)
            block = target[pl.ds(at, TSTEP), :] + target[pl.ds(at + TSTEP, TSTEP), :]
            block = jnp.transpose(block)
            target[pl.ds(at, TSTEP), :] = jnp.concatenate([block[0:TSTEP], block[TSTEP:]], axis=1)
        return carry

    lax.fori_loop(0, LEN // 2, turn, 0, unroll=8)

    finish(send_t, recv_t, 2)
    got = recv_t[:, 0, :]
    to_slot = jnp.where(lanes(owners, SLOTS).astype(F32) == got[:, 127:128] - 1.0, 1.0, 0.0)
    from_source = jnp.transpose(to_slot)
    line_traces = dot(from_source.astype(BF16), got.astype(BF16))
    filled = jnp.sum(from_source, axis=1, keepdims=True)
    place = lax.rem(lax.broadcasted_iota(jnp.int32, (SLOTS, 1), 0), LEN)
    lower = jnp.where(place > 0, filled, 0.0)
    upper = jnp.where(place < LEN - 1, pltpu.roll(jnp.broadcast_to(filled, (SLOTS, 128)), SLOTS - 1, 0)[:, 0:1], 0.0)

    def coupled(kind, gate, x):
        x = jnp.where(gate > 0.5, x, 0.0)
        spread = jnp.concatenate([x, x, x], axis=1) * chosen[kind]
        return dot(jnp.concatenate(halves(spread), axis=1), tp2[...]) * lsc[kind]

    swapped = pltpu.roll(line_traces, TSTEP, 1)
    tops = jnp.where(low_half, line_traces, swapped)
    bottoms = jnp.where(low_half, swapped, line_traces)
    terms = coupled(0, lower, pltpu.roll(tops, 1, 0)) + coupled(1, upper, pltpu.roll(bottoms, SLOTS - 1, 0))
    row_lane = lanes(LEN, 128)
    gates = jnp.where(row_lane < TSTEP, filled[0:LEN], filled[LEN:])
    gate_p[...] = jnp.broadcast_to(gates[:, None, :], (LEN, 8, 128))
    finish(send_p, recv_p, 3)
    rhs_s[...] = pick_rows(from_source, recv_p[:, 0, :]) - terms


    def trace_of_solution(given, first, gate):
        x, rows = given[...], jnp.zeros((LEN, 128), F32)
        for m in range(TRACE):
            value = jnp.broadcast_to(lane_sums(slab[3 * m + first] * x), (SLOTS, 128))
            if gate is not None:
                value = jnp.where(gate > 0.5, value, 0.0)
            store_rows(gcol, m, value)
            rows = jnp.where(row_lane == m, value[0:LEN], jnp.where(row_lane == m + TSTEP, value[LEN:], rows))
        rows_p[...] = jnp.broadcast_to(rows[:, None, :], (LEN, 8, 128))

    trace_of_solution(rhs_s, 2, None)

    send_r[:, 0, :] = pick_rows(to_slot, rhs_s[...])

    tiles = MROWS // 8
    place8 = [lax.broadcasted_iota(jnp.int32, (tiles, 8, 128), i) for i in range(3)]
    eye = jnp.where(place8[2] % TSTEP == 8 * place8[0] + place8[1], 1.0, 0.0)
    first_line = place8[2] < TSTEP

    def sweep(matrices, reverse, beside):
        def pair(i, row, last=False):
            beside(i, last)
            first = LEN - 1 - 2 * i if reverse else 2 * i
            second = first - 1 if reverse else first + 1
            at = pl.multiple_of(first * 2 * TSTEP, 128)
            column = []
            for line in range(2):
                block = pl.ds(at + line * TSTEP, MROWS)
                product = matrices[block, :].reshape(tiles, 8, 128) * row[None]
                column.append(gcol[block, :].reshape(tiles, 8, 128) - jnp.sum(product, axis=2, keepdims=True))
            column = jnp.where(first_line, column[0], column[1])
            out_p[pl.ds(first, 1), :] = jnp.sum(jnp.sum(eye * column, axis=0), axis=0, keepdims=True)
            turned = matrices[pl.ds(pl.multiple_of(second * 2 * TSTEP, 128), MROWS), :].reshape(tiles, 8, 128)
            moved = jnp.sum(jnp.sum(turned * column, axis=0), axis=0, keepdims=True)
            row = jnp.where(gate_p[second] > 0.5, rows_p[second] - moved, 0.0)
            out_p[pl.ds(second, 1), :] = row[0:1]
            return row

        pair(LEN // 2 - 1, lax.fori_loop(0, LEN // 2 - 1, pair, jnp.zeros((8, 128), F32), unroll=5), True)
        x = out_p[...]
        swapped = pltpu.roll(x, TSTEP, 1)
        low = row_lane < TSTEP
        return jnp.concatenate([jnp.where(low, x, swapped), jnp.where(low, swapped, x)], axis=0)

    def send_four(i, last):
        for other in others(i)[: 3 if last else 4]:
            send_one(send_r, back_r, 4, other)

    assert owners == 2 * LEN
    forward = sweep(mm, False, send_four)
    back_r[pl.ds(me, 1)] = send_r[pl.ds(me, 1)]

    cc[...] = rhs_s[...] - coupled(0, lower, pltpu.roll(forward, 1, 0))
    trace_of_solution(cc, 0, filled)

    backward = sweep(nn, True, lambda i, last: None)

    cc[...] = cc[...] - coupled(1, upper, pltpu.roll(backward, SLOTS - 1, 0))

    send_lane = lanes(SLOTS, WIDE)
    ret[...] = jnp.zeros((SLOTS, WIDE), F32)

    def solve(i, carry):
        total, given = ret[...], cc[...]
        for b in range(54):
            b = i * 54 + b
            total = jnp.where(send_lane == b, lane_sums(slab[b] * given), total)
        ret[...] = total
        return carry

    lax.fori_loop(0, BLOCK // 54, solve, 0)
    send_c[:, 0, :] = pick_rows(to_slot, ret[...])
    exchange(send_c, back_c, 5)
    pick_element = jnp.transpose(pick_owner)
    finish(send_r, back_r, 4)
    out[1] = rs_ref[...] - pick_rows(pick_element, back_r[:, 0, :])[0:ELEM, 0:BLOCK]
    finish(send_c, back_c, 5)
    out[0] = pick_rows(pick_element, back_c[:, 0, :])[0:ELEM, 0:BLOCK]


def local(groups, owners, flow_state, right_side, diag_block, face_scale, face_pattern, neighbour, templates, line_inverse, line_scale, line_pattern, elem_line):
    operands = (
        flow_state,
        right_side,
        diag_block,
        face_scale,
        face_pattern.T,
        neighbour.T,
        jnp.transpose(templates, (1, 0, 2)),
        line_inverse,
        line_scale,
        line_pattern.T,
        elem_line[None, :],
    )
    vmem = pl.BlockSpec(memory_space=pltpu.VMEM)
    anywhere = pl.BlockSpec(memory_space=pl.ANY)
    both = pl.pallas_call(
        functools.partial(kernel, groups, owners),
        out_shape=jax.ShapeDtypeStruct((2, ELEM, BLOCK), F32),
        in_specs=[anywhere] * 11,
        out_specs=vmem,
        scratch_shapes=[
            pltpu.VMEM((ELEM, BLOCK), F32),
            pltpu.VMEM((ELEM, BLOCK), F32),
            pltpu.VMEM((ELEM, 4, BLOCK), BF16),
            pltpu.VMEM((4, ELEM), jnp.int32),
            pltpu.VMEM((4, ELEM), jnp.int32),
            pltpu.VMEM((NPAT, TRACE, BLOCK), BF16),
            pltpu.VMEM((SLOTS, 2, BLOCK), BF16),
            pltpu.VMEM((2, SLOTS), jnp.int32),
            pltpu.VMEM((1, ELEM), jnp.int32),
            pltpu.VMEM((ELEM, BLOCK * BLOCK), BF16),
            pltpu.VMEM((SLOTS, BLOCK * BLOCK), BF16),
            pltpu.VMEM((16, 128), F32),
            pltpu.VMEM((EROWS, WIDE), F32),
            pltpu.VMEM((3, EROWS, WIDE), BF16),
            pltpu.VMEM((TALL, WIDE), F32),
            pltpu.VMEM((TALL, WIDE), BF16),
            pltpu.VMEM((2 * TALL, WIDE), BF16),
            pltpu.VMEM((2 * WIDE, TALL), BF16),
            pltpu.VMEM((4, EROWS, WIDE), F32),
            pltpu.VMEM((2, SLOTS, WIDE), F32),
            pltpu.VMEM((4, WIDE, TALL), BF16),
            pltpu.VMEM((WIDE, 128), BF16),
            pltpu.VMEM((BLOCK, SLOTS, WIDE), F32),
            pltpu.VMEM((SLOTS * TSTEP, 128), F32),
            pltpu.VMEM((SLOTS * TSTEP, 128), F32),
            pltpu.VMEM((EROWS, WIDE), F32),
            pltpu.VMEM((SLOTS * TSTEP, 128), F32),
            pltpu.VMEM((LEN, 8, 128), F32),
            pltpu.VMEM((LEN, 8, 128), F32),
            pltpu.VMEM((LEN, 128), F32),
            pltpu.VMEM((SLOTS, WIDE), F32),
            pltpu.VMEM((SLOTS, WIDE), F32),
            *[pltpu.VMEM((owners, 1, width), F32) for width in (128, 128) + (WIDE,) * 6],
            pltpu.VMEM((SLOTS, WIDE), F32),
            pltpu.SemaphoreType.DMA((2 + 9,)),
            pltpu.SemaphoreType.DMA((6,)),
            pltpu.SemaphoreType.DMA((6,)),
        ],
        compiler_params=pltpu.CompilerParams(collective_id=0, has_side_effects=True, vmem_limit_bytes=56 * 1024 * 1024),
    )(*operands)
    return flow_state + both[0], right_side - both[1]


def solution(mesh):
    both = ("region", "dom")
    return jax.shard_map(
        functools.partial(local, mesh.shape["region"], mesh.shape["dom"]),
        mesh=mesh,
        in_specs=(
            P(both, None),
            P(both, None),
            P(both, None),
            P(both, None, None),
            P(both, None),
            P(both, None),
            P(),
            P(both, None),
            P(both, None, None),
            P(both, None),
            P(both),
        ),
        out_specs=(P(both, None), P(both, None)),
        check_vma=False,
    )
```

```python
import functools

import jax
import jax.numpy as jnp
import numpy as np
from jax import lax
from jax.experimental import pallas as pl
from jax.experimental.pallas import tpu as pltpu
from jax.sharding import PartitionSpec as P

MESH = pl.DeviceIdType.MESH
F32, BF16 = jnp.float32, jnp.bfloat16
OPPOSITE = (1, 0, 3, 2)

NV = 6
NPAT = 6
LEN = 32
BLOCK = 162
TRACE = 54
ELEM = 26
SLOTS = 64
EROWS = 32
WIDE = 256
TSTEP = 64
TALL = NPAT * TSTEP
MROWS = 56


def trace_column(face_id, width):
    k = lax.rem(lanes(1, width), TSTEP).astype(F32)
    variable, rest = jnp.floor((k + 0.5) * (1.0 / 9.0)), 0.0
    line = jnp.floor((k + 0.5) * (1.0 / 3.0))
    if face_id < 2:
        rest = k + 18.0 * variable + 18.0 * face_id
    elif face_id < 4:
        rest = k + 6.0 * line + 6.0 * (face_id - 2)
    else:
        rest = 3.0 * k + 2.0 * (face_id - 4)
    return jnp.where(k < TRACE, rest, -1.0)


def picks_of(column):
    rows = lax.broadcasted_iota(jnp.int32, (WIDE, column.shape[1]), 0).astype(F32)
    return jnp.where(rows == column, 1.0, 0.0).astype(BF16)


def dot(a, b):
    return jnp.dot(a, b, preferred_element_type=F32)


def lanes(rows, width):
    return lax.broadcasted_iota(jnp.int32, (rows, width), 1)


def pick_rows(pick, x):
    pick = pick.astype(BF16)
    return dot(jnp.concatenate([pick, pick], axis=1), jnp.concatenate(halves(x), axis=0))


def halves(x):
    high = x.astype(BF16)
    return high, (x - high.astype(F32)).astype(BF16)


def block_row(ref, rows, start):
    base = pl.multiple_of((start // 128) * 128, 128)
    shift = lax.rem(128 - (start - base), 128)
    tiles = [ref[0:rows, pl.ds(pl.multiple_of(base + 128 * t, 128), 128)].astype(F32) for t in range(3)]
    moved = [pltpu.roll(tile, shift, 1) for tile in tiles]
    keep = lanes(rows, 128) < 128 - (start - base)
    return jnp.concatenate([jnp.where(keep, moved[0], moved[1]), jnp.where(keep, moved[1], moved[2])], axis=1)


def lane_sums(product):
    return jnp.sum(product[:, 0:128] + product[:, 128:256], axis=1, keepdims=True)


def kernel(
    groups,
    owners,
    fs_hbm,
    rs_hbm,
    diag_hbm,
    fsc_hbm,
    fp_hbm,
    nb_hbm,
    tmpl_hbm,
    linv_hbm,
    lsc_hbm,
    lp_hbm,
    el_hbm,
    out,
    fs_ref,
    rs_ref,
    fsc_ref,
    fp_ref,
    nb_ref,
    tmpl_ref,
    lsc_ref,
    lp_ref,
    el_ref,
    diag,
    linv,
    ints,
    xs,
    st,
    tf,
    tp,
    tp2,
    tpt,
    fsc,
    lsc,
    picks,
    lpick,
    slab,
    mm,
    nn,
    own,
    gcol,
    rows_p,
    gate_p,
    out_p,
    cc,
    rhs_s,
    send_t,
    recv_t,
    send_p,
    recv_p,
    send_r,
    back_r,
    send_c,
    back_c,
    ret,
    dsem,
    ssem,
    rsem,
):
    reg = lax.axis_index("region")
    me = lax.axis_index("dom")

    bar = pltpu.get_barrier_semaphore()
    below, above = lax.rem(reg + groups - 1, groups), lax.rem(reg + 1, groups)

    def others(i):
        far = owners // 8
        dz = jnp.where(lax.rem(i, 2) == 1, far - (i + 1) // 2, far + i // 2)
        z = lax.rem(me // 4 + dz, owners // 4)
        return [z * 4 + lax.rem(me + dx, 4) for dx in (2, 1, 3, 0)]

    def greet(i, carry):
        for other in others(i):
            pl.semaphore_signal(bar, inc=1, device_id=(reg, other), device_id_type=MESH)
        return carry

    pl.semaphore_signal(bar, inc=1, device_id=(below, me), device_id_type=MESH)
    pl.semaphore_signal(bar, inc=1, device_id=(above, me), device_id_type=MESH)
    lax.fori_loop(0, owners // 4 - 1, greet, 0)
    for other in others(owners // 4 - 1)[:3]:
        pl.semaphore_signal(bar, inc=1, device_id=(reg, other), device_id_type=MESH)
    get_diag = pltpu.make_async_copy(diag_hbm, diag, dsem.at[0])
    get_linv = pltpu.make_async_copy(linv_hbm, linv, dsem.at[1])
    small = ((fs_hbm, fs_ref), (tmpl_hbm, tmpl_ref), (nb_hbm, nb_ref), (fp_hbm, fp_ref), (el_hbm, el_ref), (lp_hbm, lp_ref), (fsc_hbm, fsc_ref), (lsc_hbm, lsc_ref), (rs_hbm, rs_ref))
    fetches = [pltpu.make_async_copy(source, target, dsem.at[2 + i]) for i, (source, target) in enumerate(small)]
    for fetch in fetches:
        fetch.start()
    get_diag.start()
    get_linv.start()
    for fetch in fetches:
        fetch.wait()

    ints[...] = jnp.full((16, 128), -1.0, F32)
    ints[0:4, 0:ELEM] = nb_ref[...].astype(F32)
    ints[4:8, 0:ELEM] = fp_ref[...].astype(F32)
    ints[8:9, 0:ELEM] = el_ref[...].astype(F32)
    ints[9:11, 0:SLOTS] = lp_ref[...].astype(F32)
    columns = jnp.transpose(ints[...])

    xs[...] = jnp.zeros((EROWS, WIDE), F32)
    xs[0:ELEM, 0:BLOCK] = fs_ref[...]
    rounded = xs[...].astype(BF16)
    st[1] = rounded
    wide_state = rounded.astype(F32)

    tf[...] = jnp.zeros((TALL, WIDE), F32)
    for pattern in range(NPAT):
        tf[pattern * TSTEP : pattern * TSTEP + TRACE, 0:BLOCK] = tmpl_ref[pattern].astype(F32)
    tp[...] = tf[...].astype(BF16)
    turned = jnp.transpose(tf[...]).astype(BF16)
    tp2[0:TALL] = tp[...]
    tp2[TALL:] = tp[...]
    tpt[0:WIDE] = turned
    tpt[WIDE:] = turned
    fsc[...] = jnp.zeros((4, EROWS, WIDE), F32)
    for side in range(4):
        fsc[side, 0:ELEM, 0:BLOCK] = fsc_ref[:, side, :].astype(F32)
    lsc[...] = jnp.zeros((2, SLOTS, WIDE), F32)
    for side in range(2):
        lsc[side, :, 0:BLOCK] = lsc_ref[:, side, :].astype(F32)

    for side in range(4):
        picks[side] = picks_of(trace_column(OPPOSITE[side], TALL))
    lpick[...] = picks_of(jnp.where(lanes(1, 128) < TSTEP, trace_column(5, 128), trace_column(4, 128)))

    get_diag.wait()

    def own_rows_of(i, carry):
        for b in range(23):
            slab[i * 23 + b, 0:ELEM] = block_row(diag, ELEM, (i * 23 + b) * BLOCK)
        return carry

    lax.fori_loop(0, (BLOCK - 1) // 23, own_rows_of, 0)
    tail = diag[:, (BLOCK - 1) * BLOCK - 98 : BLOCK * BLOCK].astype(F32)
    slab[BLOCK - 1, 0:EROWS] = jnp.zeros((EROWS, WIDE), F32)
    slab[BLOCK - 1, 0:ELEM, 0:BLOCK] = tail[:, 98 : 98 + BLOCK]
    own[...] = jnp.zeros((EROWS, WIDE), F32)
    elem_lane = lanes(EROWS, WIDE)

    def own_rows(i, carry):
        total = own[...]
        for b in range(54):
            b = i * 54 + b
            total = jnp.where(elem_lane == b, lane_sums(slab[b, 0:EROWS] * wide_state), total)
        own[...] = total
        return carry

    lax.fori_loop(0, BLOCK // 54, own_rows, 0)

    get_linv.wait()

    def rows_of(i, carry):
        for b in range(23):
            slab[i * 23 + b] = block_row(linv, SLOTS, (i * 23 + b) * BLOCK)
        return carry

    lax.fori_loop(0, (BLOCK - 1) // 23, rows_of, 0)
    tail = linv[:, (BLOCK - 1) * BLOCK - 98 : BLOCK * BLOCK].astype(F32)
    slab[BLOCK - 1] = jnp.zeros((SLOTS, WIDE), F32)
    slab[BLOCK - 1, :, 0:BLOCK] = tail[:, 98 : 98 + BLOCK]

    slot = columns[0:EROWS, 8:9]
    local_slot = slot - jnp.floor(slot * (1.0 / SLOTS)) * SLOTS
    traces = dot(rounded, lpick[...])
    traces = jnp.where(lanes(EROWS, 128) == 127, local_slot + 1.0, traces)
    owner_row = jnp.floor(ints[8:9, 0:EROWS] * (1.0 / SLOTS))
    pick_owner = jnp.where(lax.broadcasted_iota(jnp.int32, (owners, EROWS), 0).astype(F32) == owner_row, 1.0, 0.0)
    send_t[:, 0, :] = dot(pick_owner.astype(BF16), traces.astype(BF16))

    def send_one(source, target, index, other):
        pltpu.make_async_remote_copy(
            src_ref=source.at[other],
            dst_ref=target.at[me],
            send_sem=ssem.at[index],
            recv_sem=rsem.at[index],
            device_id=(reg, other),
            device_id_type=MESH,
        ).start()

    def exchange(source, target, index):
        def four(i, carry):
            for other in others(i):
                send_one(source, target, index, other)
            return carry

        lax.fori_loop(0, owners // 4 - 1, four, 0)
        for other in others(owners // 4 - 1)[:3]:
            send_one(source, target, index, other)
        target[pl.ds(me, 1)] = source[pl.ds(me, 1)]

    def finish(source, target, index):
        whole = pltpu.make_async_remote_copy(
            src_ref=source.at[pl.ds(0, owners - 1)],
            dst_ref=target.at[pl.ds(0, owners - 1)],
            send_sem=ssem.at[index],
            recv_sem=rsem.at[index],
            device_id=(reg, lax.rem(me + 1, owners)),
            device_id_type=MESH,
        )
        whole.wait_send()
        whole.wait_recv()

    kinds = [columns[0:SLOTS, 9 + i : 10 + i] for i in range(2)]
    chosen = [jnp.where((lanes(SLOTS, TALL) // TSTEP).astype(F32) == kind, 1.0, 0.0) for kind in kinds]
    low_half = lanes(SLOTS, 128) < TSTEP
    own_half = lanes(SLOTS, 128) // TSTEP == lax.broadcasted_iota(jnp.int32, (SLOTS, 128), 0) // LEN

    def store_rows(target, m, x):
        target[pl.ds(m, LEN, stride=2 * TSTEP), :] = x[0:LEN]
        target[pl.ds(m + TSTEP, LEN, stride=2 * TSTEP), :] = x[LEN:]

    def small_rows(i, carry):
        parts = []
        for u in range(9):
            m = 9 * i + u
            for x in (slab[3 * m + 2] * lsc[0], slab[3 * m] * lsc[1]):
                parts.append(jnp.concatenate(halves(x), axis=1))
        product = dot(jnp.concatenate(parts, axis=0), tpt[...])
        for u in range(9):
            for kind, target in enumerate((mm, nn)):
                at = (u * 2 + kind) * SLOTS
                x = product[at : at + SLOTS] * chosen[kind]
                x = x[:, 0:128] + x[:, 128:256] + x[:, 256:384]
                x = x + pltpu.roll(x, TSTEP, 1)
                store_rows(target, 9 * i + u, jnp.where(own_half, x, 0.0))
        return carry

    pl.semaphore_wait(bar, owners + 1)
    up = pltpu.make_async_remote_copy(
        src_ref=st.at[1], dst_ref=st.at[0], send_sem=ssem.at[0], recv_sem=rsem.at[0], device_id=(above, me), device_id_type=MESH
    )
    down = pltpu.make_async_remote_copy(
        src_ref=st.at[1], dst_ref=st.at[2], send_sem=ssem.at[1], recv_sem=rsem.at[1], device_id=(below, me), device_id_type=MESH
    )
    up.start()
    down.start()
    exchange(send_t, recv_t, 2)
    lax.fori_loop(0, 3, small_rows, 0)
    up.wait()
    down.wait()

    stacked = jnp.concatenate([st[0], st[1], st[2]], axis=0)
    row_lane = lanes(EROWS, 3 * EROWS).astype(F32)
    has_below = jnp.where(reg > 0, 1.0, 0.0)
    has_above = jnp.where(reg < groups - 1, 1.0, 0.0)
    pieces = []
    for side in range(4):
        near = columns[0:EROWS, side : side + 1]
        part = jnp.where(near >= ELEM, 1.0, 0.0) + jnp.where(near >= 2 * ELEM, 1.0, 0.0)
        place = near + (EROWS - ELEM) * part
        present = jnp.where(part == 0.0, has_below, jnp.where(part == 2.0, has_above, 1.0))
        pick = jnp.where(row_lane == place, present, 0.0).astype(BF16)
        fetched = dot(pick, stacked).astype(BF16)
        spread = dot(fetched, picks[side])
        pattern = columns[0:EROWS, 4 + side : 5 + side]
        pieces.append(jnp.where((lanes(EROWS, TALL) // TSTEP).astype(F32) == pattern, spread, 0.0).astype(BF16))
    terms = dot(jnp.concatenate(pieces, axis=0), tp[...])
    total = own[...]
    for side in range(4):
        total = total + terms[side * EROWS : (side + 1) * EROWS] * fsc[side]
    xs[...] = jnp.zeros((EROWS, WIDE), F32)
    xs[0:ELEM, 0:BLOCK] = rs_ref[...]
    send_p[:, 0, :] = pick_rows(pick_owner, xs[...] - total)
    exchange(send_p, recv_p, 3)

    lax.fori_loop(3, TRACE // 9, small_rows, 0)
    for m in range(TRACE, TSTEP):
        for target in (mm, nn, gcol):
            store_rows(target, m, jnp.zeros((SLOTS, 128), F32))

    def turn(i, carry):
        for target, position in ((mm, 2 * i + 1), (nn, 2 * i)):
            at = pl.multiple_of(position * 2 * TSTEP, 128)
            block = target[pl.ds(at, TSTEP), :] + target[pl.ds(at + TSTEP, TSTEP), :]
            block = jnp.transpose(block)
            target[pl.ds(at, TSTEP), :] = jnp.concatenate([block[0:TSTEP], block[TSTEP:]], axis=1)
        return carry

    lax.fori_loop(0, LEN // 2, turn, 0, unroll=8)

    finish(send_t, recv_t, 2)
    got = recv_t[:, 0, :]
    to_slot = jnp.where(lanes(owners, SLOTS).astype(F32) == got[:, 127:128] - 1.0, 1.0, 0.0)
    from_source = jnp.transpose(to_slot)
    line_traces = dot(from_source.astype(BF16), got.astype(BF16))
    filled = jnp.sum(from_source, axis=1, keepdims=True)
    place = lax.rem(lax.broadcasted_iota(jnp.int32, (SLOTS, 1), 0), LEN)
    lower = jnp.where(place > 0, filled, 0.0)
    upper = jnp.where(place < LEN - 1, pltpu.roll(jnp.broadcast_to(filled, (SLOTS, 128)), SLOTS - 1, 0)[:, 0:1], 0.0)

    def coupled(kind, gate, x):
        x = jnp.where(gate > 0.5, x, 0.0)
        spread = jnp.concatenate([x, x, x], axis=1) * chosen[kind]
        return dot(jnp.concatenate(halves(spread), axis=1), tp2[...]) * lsc[kind]

    swapped = pltpu.roll(line_traces, TSTEP, 1)
    tops = jnp.where(low_half, line_traces, swapped)
    bottoms = jnp.where(low_half, swapped, line_traces)
    terms = coupled(0, lower, pltpu.roll(tops, 1, 0)) + coupled(1, upper, pltpu.roll(bottoms, SLOTS - 1, 0))
    row_lane = lanes(LEN, 128)
    gates = jnp.where(row_lane < TSTEP, filled[0:LEN], filled[LEN:])
    gate_p[...] = jnp.broadcast_to(gates[:, None, :], (LEN, 8, 128))
    finish(send_p, recv_p, 3)
    rhs_s[...] = pick_rows(from_source, recv_p[:, 0, :]) - terms


    def trace_of_solution(given, first, gate):
        x, rows = given[...], jnp.zeros((LEN, 128), F32)
        for m in range(TRACE):
            value = jnp.broadcast_to(lane_sums(slab[3 * m + first] * x), (SLOTS, 128))
            if gate is not None:
                value = jnp.where(gate > 0.5, value, 0.0)
            store_rows(gcol, m, value)
            rows = jnp.where(row_lane == m, value[0:LEN], jnp.where(row_lane == m + TSTEP, value[LEN:], rows))
        rows_p[...] = jnp.broadcast_to(rows[:, None, :], (LEN, 8, 128))

    trace_of_solution(rhs_s, 2, None)

    send_r[:, 0, :] = pick_rows(to_slot, rhs_s[...])

    tiles = MROWS // 8
    place8 = [lax.broadcasted_iota(jnp.int32, (tiles, 8, 128), i) for i in range(3)]
    eye = jnp.where(place8[2] % TSTEP == 8 * place8[0] + place8[1], 1.0, 0.0)
    first_line = place8[2] < TSTEP

    def steps(matrices, reverse, beside):
        def pair(i, row, last=False):
            beside(i, last)
            first = LEN - 1 - 2 * i if reverse else 2 * i
            second = first - 1 if reverse else first + 1
            at = pl.multiple_of(first * 2 * TSTEP, 128)
            column = []
            for line in range(2):
                block = pl.ds(at + line * TSTEP, MROWS)
                product = matrices[block, :].reshape(tiles, 8, 128) * row[None]
                column.append(gcol[block, :].reshape(tiles, 8, 128) - jnp.sum(product, axis=2, keepdims=True))
            column = jnp.where(first_line, column[0], column[1])
            out_p[pl.ds(first, 1), :] = jnp.sum(jnp.sum(eye * column, axis=0), axis=0, keepdims=True)
            turned = matrices[pl.ds(pl.multiple_of(second * 2 * TSTEP, 128), MROWS), :].reshape(tiles, 8, 128)
            moved = jnp.sum(jnp.sum(turned * column, axis=0), axis=0, keepdims=True)
            row = jnp.where(gate_p[second] > 0.5, rows_p[second] - moved, 0.0)
            out_p[pl.ds(second, 1), :] = row[0:1]
            return row

        return pair

    def both_halves(x):
        swapped = pltpu.roll(x, TSTEP, 1)
        low = lanes(x.shape[0], 128) < TSTEP
        return jnp.concatenate([jnp.where(low, x, swapped), jnp.where(low, swapped, x)], axis=0)

    nothing = jnp.zeros((8, 128), F32)

    def send_four(i, last):
        for other in others(i)[: 3 if last else 4]:
            send_one(send_r, back_r, 4, other)

    assert owners == 2 * LEN
    pair = steps(mm, False, send_four)
    pair(LEN // 2 - 1, lax.fori_loop(0, LEN // 2 - 1, pair, nothing, unroll=5), True)
    forward = both_halves(out_p[...])
    back_r[pl.ds(me, 1)] = send_r[pl.ds(me, 1)]

    cc[...] = rhs_s[...] - coupled(0, lower, pltpu.roll(forward, 1, 0))
    trace_of_solution(cc, 0, filled)

    half = LEN // 2

    def part(x, high):
        start = half if high else 0
        return jnp.concatenate([x[start : start + half], x[start + LEN : start + LEN + half]], axis=0)

    def finished(high, after):
        x = jnp.where(part(upper, high) > 0.5, after, 0.0)
        spread = jnp.concatenate([x, x, x], axis=1) * part(chosen[1], high)
        term = dot(jnp.concatenate(halves(spread), axis=1), tp2[...]) * part(lsc[1], high)
        return part(cc[...], high) - term

    half_lane = lanes(LEN, WIDE)

    def solve(b, given, high, total):
        start = half if high else 0
        rows = jnp.concatenate([slab[b, start : start + half], slab[b, start + LEN : start + LEN + half]], axis=0)
        return jnp.where(half_lane == b, lane_sums(rows * given), total)

    pair = steps(nn, True, lambda i, last: None)
    row = lax.fori_loop(0, half // 2, pair, nothing, unroll=4)
    given = finished(True, pltpu.roll(both_halves(out_p[half:LEN]), LEN - 1, 0))
    total = jnp.zeros((LEN, WIDE), F32)
    for i in range(half // 2):
        row = pair(half // 2 + i, row)
        for b in range(BLOCK * i // (half // 2), BLOCK * (i + 1) // (half // 2)):
            total = solve(b, given, True, total)
    ret[half:LEN] = total[0:half]
    ret[half + LEN : 2 * LEN] = total[half:]

    given = finished(False, both_halves(out_p[1 : half + 1]))
    total = jnp.zeros((LEN, WIDE), F32)
    for b in range(BLOCK):
        total = solve(b, given, False, total)
    ret[0:half] = total[0:half]
    ret[LEN : LEN + half] = total[half:]

    send_c[:, 0, :] = pick_rows(to_slot, ret[...])
    exchange(send_c, back_c, 5)
    pick_element = jnp.transpose(pick_owner)
    finish(send_r, back_r, 4)
    out[1] = rs_ref[...] - pick_rows(pick_element, back_r[:, 0, :])[0:ELEM, 0:BLOCK]
    finish(send_c, back_c, 5)
    out[0] = pick_rows(pick_element, back_c[:, 0, :])[0:ELEM, 0:BLOCK]


def local(groups, owners, flow_state, right_side, diag_block, face_scale, face_pattern, neighbour, templates, line_inverse, line_scale, line_pattern, elem_line):
    operands = (
        flow_state,
        right_side,
        diag_block,
        face_scale,
        face_pattern.T,
        neighbour.T,
        jnp.transpose(templates, (1, 0, 2)),
        line_inverse,
        line_scale,
        line_pattern.T,
        elem_line[None, :],
    )
    vmem = pl.BlockSpec(memory_space=pltpu.VMEM)
    anywhere = pl.BlockSpec(memory_space=pl.ANY)
    both = pl.pallas_call(
        functools.partial(kernel, groups, owners),
        out_shape=jax.ShapeDtypeStruct((2, ELEM, BLOCK), F32),
        in_specs=[anywhere] * 11,
        out_specs=vmem,
        scratch_shapes=[
            pltpu.VMEM((ELEM, BLOCK), F32),
            pltpu.VMEM((ELEM, BLOCK), F32),
            pltpu.VMEM((ELEM, 4, BLOCK), BF16),
            pltpu.VMEM((4, ELEM), jnp.int32),
            pltpu.VMEM((4, ELEM), jnp.int32),
            pltpu.VMEM((NPAT, TRACE, BLOCK), BF16),
            pltpu.VMEM((SLOTS, 2, BLOCK), BF16),
            pltpu.VMEM((2, SLOTS), jnp.int32),
            pltpu.VMEM((1, ELEM), jnp.int32),
            pltpu.VMEM((ELEM, BLOCK * BLOCK), BF16),
            pltpu.VMEM((SLOTS, BLOCK * BLOCK), BF16),
            pltpu.VMEM((16, 128), F32),
            pltpu.VMEM((EROWS, WIDE), F32),
            pltpu.VMEM((3, EROWS, WIDE), BF16),
            pltpu.VMEM((TALL, WIDE), F32),
            pltpu.VMEM((TALL, WIDE), BF16),
            pltpu.VMEM((2 * TALL, WIDE), BF16),
            pltpu.VMEM((2 * WIDE, TALL), BF16),
            pltpu.VMEM((4, EROWS, WIDE), F32),
            pltpu.VMEM((2, SLOTS, WIDE), F32),
            pltpu.VMEM((4, WIDE, TALL), BF16),
            pltpu.VMEM((WIDE, 128), BF16),
            pltpu.VMEM((BLOCK, SLOTS, WIDE), F32),
            pltpu.VMEM((SLOTS * TSTEP, 128), F32),
            pltpu.VMEM((SLOTS * TSTEP, 128), F32),
            pltpu.VMEM((EROWS, WIDE), F32),
            pltpu.VMEM((SLOTS * TSTEP, 128), F32),
            pltpu.VMEM((LEN, 8, 128), F32),
            pltpu.VMEM((LEN, 8, 128), F32),
            pltpu.VMEM((LEN, 128), F32),
            pltpu.VMEM((SLOTS, WIDE), F32),
            pltpu.VMEM((SLOTS, WIDE), F32),
            *[pltpu.VMEM((owners, 1, width), F32) for width in (128, 128) + (WIDE,) * 6],
            pltpu.VMEM((SLOTS, WIDE), F32),
            pltpu.SemaphoreType.DMA((2 + 9,)),
            pltpu.SemaphoreType.DMA((6,)),
            pltpu.SemaphoreType.DMA((6,)),
        ],
        compiler_params=pltpu.CompilerParams(collective_id=0, has_side_effects=True, vmem_limit_bytes=56 * 1024 * 1024),
    )(*operands)
    return flow_state + both[0], right_side - both[1]


def solution(mesh):
    both = ("region", "dom")
    return jax.shard_map(
        functools.partial(local, mesh.shape["region"], mesh.shape["dom"]),
        mesh=mesh,
        in_specs=(
            P(both, None),
            P(both, None),
            P(both, None),
            P(both, None, None),
            P(both, None),
            P(both, None),
            P(),
            P(both, None),
            P(both, None, None),
            P(both, None),
            P(both),
        ),
        out_specs=(P(both, None), P(both, None)),
        check_vma=False,
    )
```
